128 devices in a mesh: dp: 16 (over x, z), tensor: 8 (over y, core).
Axes of the slice: x: 4, y: 4, z: 4, core: 2. Of those that a mesh axis runs over, the one named last changes fastest.
Arguments:
- embeddings: bfloat16 [8192, 2048], P('dp', 'tensor'), may hold values from -6 to 6
- trunk_weights: bfloat16 [2, 2048, 2048], P(None, None, 'tensor'), may hold values from -0.125 to 0.125
- trunk_gains: float32 [2, 2048], replicated, may hold values from 0.1 to 1.9
- expert_weights: bfloat16 [8, 2048, 2048], P('tensor'), may hold values from -0.125 to 0.125
- route_ids: int32 [8192, 2], P('dp'), may hold values from 0 to 7, all different within a row; in each aligned block of 512 rows (0 to 511, 512 to 1023, ...) at most 256 rows name the same one
- task_gates: float32 [8192, 2, 2], P('dp'), may hold values from 0.2 to 1
- mixture_grad: bfloat16 [2, 8192, 2048], P(None, 'dp', 'tensor'), may hold values from -0.119628906 to 0.119628906
Outputs:
- task_mixture: bfloat16 [2, 8192, 2048], P(None, 'dp', 'tensor')
- expert_grad: float32 [8, 2048, 2048], P('tensor', 'dp')
The draws below stay inside these ranges and needn't reach their ends.
Inputs may be any that keep to these rules, and one draw needn't show every extreme that they name: `route_ids`: the 2 experts of an example differ. In each aligned block of 512 examples (the examples of one index of dp) no expert is chosen more than 256 times, and some expert is chosen exactly 256 times in some block.
All inputs are finite; a program needn't handle non-finite values.
Results may differ from the reference program's by a relative error of at most 0.014.
Values may be sent and summed in bfloat16 or wider, within the bound.
A program may use at most 128 MiB of HBM per device.

```python
import functools
import math
import jax
import jax.numpy as jnp
import numpy as np
from jax import lax

NEMB = 16
DEMB = 128
H = 2048
TOP = 2
TASKS = 2
NBLK = 2
ROWS_DEV = 512
D = 2048
EXPERTS = 8
CAP = 256
BATCH = 8192
N_DP = 16


def block_scale(stream_key, dims, pieces, least, largest):
    loudness = 1.0
    for position, parts in pieces:
        draws = jax.random.uniform(jax.random.fold_in(jax.random.fold_in(stream_key, 6), position), (parts,), jnp.float32, least / len(pieces), largest / len(pieces))
        loudness = loudness * jnp.repeat(jnp.exp(draws), dims[position] // parts).reshape((-1,) + (1,) * (len(dims) - 1 - position))
    return loudness


def assign_block(key, own, number, rows, count, top, reach, lean):
    sequence = jax.random.permutation(key, count)
    heavy_load, usual = shares(count, rows * top, reach, lean, True), shares(count, rows * top, reach, lean, False)
    places = jnp.arange(count)

    def named(tallies, turn):
        used = int((tallies > 0).sum())
        fixed = max(1, used // 4)
        passed = fixed + (places - fixed + turn * (used - fixed)) % max(1, count - fixed)
        return jnp.zeros((count,), jnp.int32).at[sequence[jnp.where(places < fixed, places, passed)]].set(jnp.asarray(tallies, jnp.int32))

    tallies = jnp.where(number % 4 == 0, named(heavy_load, number // 4), named(usual, number - number // 4 - 1))
    mixed = jax.random.permutation(jax.random.fold_in(own, 3), count)
    source_of, taker = mixed[0:count // 2 * 2:2], mixed[1:count // 2 * 2:2]
    margin = jnp.minimum(tallies[source_of] - 1, reach - tallies[taker]) // 2
    margin = jnp.where((source_of == sequence[0]) | (taker == sequence[0]) | (tallies[taker] == 0), 0, jnp.maximum(margin, 0))
    passed = jax.random.randint(jax.random.fold_in(own, 4), (count // 2,), 0, 1 << 20) % (margin + 1)
    tallies = tallies.at[source_of].add(-passed).at[taker].add(passed)
    members = jnp.searchsorted(jnp.cumsum(tallies), jnp.arange(rows * top), side="right").astype(jnp.int32)
    listing = members.reshape(top, rows).T
    listing = listing[jax.random.permutation(jax.random.fold_in(own, 1), rows)]
    turn = jax.random.randint(jax.random.fold_in(own, 2), (rows, 1), 0, top)
    return jnp.take_along_axis(listing, (jnp.arange(top)[None, :] + turn) % top, axis=1)


def shares(amount, total, most, slope, full):
    loads = [(1 << 20) // math.isqrt(grade ** slope) + 1 for grade in range(1, amount + 1)]
    largest = most if full else min(most, max(-(-total // amount), total * loads[0] // sum(loads)))
    least = 1 if total - largest >= amount - 1 else 0
    given, spare = [largest] + [least] * (amount - 1), total - largest - least * (amount - 1)
    while spare > 0:
        free = [i for i in range(1, amount) if given[i] < largest] or [i for i in range(1, amount) if given[i] < most]
        pool, left = sum([loads[i] for i in free]), spare
        for i in free:
            addition = min(most - given[i], max(1, left * loads[i] // pool), spare)
            given[i] = given[i] + addition
            spare = spare - addition
    return np.array(given)


def centred(stream_key, extent, spread, most, pieces=(), kind=jnp.bfloat16):
    array = jax.random.normal(stream_key, extent, jnp.float32) * spread
    if len(pieces) > 0:
        array = block_scale(stream_key, extent, pieces, -0.22, 0.18) * array
    return jnp.clip(array, min=-most, max=most).astype(kind)


def setup_inputs(seed: int = 0) -> dict:
    key_list = jax.random.split(jax.random.key(seed), 8)
    embeddings = centred(key_list[0], (BATCH, D), 1.0, 6.0, ((0, 16), (1, 8)))
    trunk_weights = centred(key_list[1], (NBLK, D, D), D ** -0.5, 0.125, ((2, 8),))
    trunk_gains = jnp.clip(1.0 + 0.18 * jax.random.normal(key_list[2], (NBLK, D), jnp.float32), 0.1, 1.9)
    expert_weights = centred(key_list[3], (EXPERTS, D, H), D ** -0.5, 0.125, ((0, 8),))
    route_ids_keys = jax.random.split(jax.random.fold_in(key_list[4], 1), BATCH // ROWS_DEV)
    route_ids_turns = jax.random.permutation(jax.random.fold_in(key_list[4], 3), BATCH // ROWS_DEV)
    route_ids = jax.vmap(lambda own, number: assign_block(jax.random.fold_in(key_list[4], 2), own, number, ROWS_DEV, EXPERTS, TOP, CAP, 2))(route_ids_keys, route_ids_turns).reshape((BATCH, TOP))
    task_gates = jnp.clip(0.2 + 0.8 * jax.random.uniform(key_list[5], (BATCH, TASKS, TOP), jnp.float32) ** block_scale(key_list[5], (BATCH, TASKS, TOP), ((0, 16),), -0.2, 0.2), 0.2, 1.0)
    mixture_grad = centred(key_list[6], (TASKS, BATCH, H), 0.02, 0.119628906, ((1, 16), (2, 8)))
    return {"embeddings": embeddings, "trunk_weights": trunk_weights, "trunk_gains": trunk_gains, "expert_weights": expert_weights, "route_ids": route_ids, "task_gates": task_gates, "mixture_grad": mixture_grad}


def silu_grad(pre_act):
    sigma = jax.nn.sigmoid(pre_act)
    return sigma + pre_act * sigma * (1.0 - sigma)

def slot_tables(route_block, experts, capacity):
    flat_ids = route_block.reshape(-1).astype(jnp.int32)
    count = flat_ids.shape[0]
    onehot = (flat_ids[:, None] == jnp.arange(experts, dtype=jnp.int32)[None, :]).astype(jnp.int32)
    running = (jnp.cumsum(onehot, axis=0) - 1).astype(jnp.int32)
    place = lax.optimization_barrier(jnp.sum(onehot * running, axis=1)).astype(jnp.int32)
    slot_index = (flat_ids * capacity + place).astype(jnp.int32)
    slot_source = jnp.full((experts * capacity,), count, jnp.int32).at[slot_index].set(jnp.arange(count, dtype=jnp.int32))
    return (slot_index, slot_source)

def interaction(whole, gain):
    wide = whole.astype(jnp.float32)
    scale = lax.rsqrt(lax.optimization_barrier(jnp.mean(wide * wide, axis=1, keepdims=True)) + 1e-05)
    normed = (wide * scale * gain[None, :]).astype(jnp.bfloat16)
    cube = normed.reshape(normed.shape[0], NEMB, DEMB)
    gram = jnp.einsum('rnd,rmd->rnm', cube, cube, preferred_element_type=jnp.float32) / math.sqrt(DEMB)
    inter = jnp.einsum('rnm,rmd->rnd', gram, cube.astype(jnp.float32), precision=lax.Precision.HIGHEST) / math.sqrt(NEMB)
    return inter.reshape(whole.shape[0], NEMB * DEMB).astype(jnp.bfloat16)

def reference(embeddings, trunk_weights, trunk_gains, expert_weights, route_ids, task_gates, mixture_grad):
    trunk = embeddings
    for block_index in range(NBLK):
        inter = interaction(trunk, trunk_gains[block_index])
        branch = jax.nn.silu(jnp.dot(inter, trunk_weights[block_index], preferred_element_type=jnp.float32))
        trunk = (trunk.astype(jnp.float32) + branch).astype(jnp.bfloat16)
    count = ROWS_DEV * TOP
    blocks = route_ids.reshape(N_DP, count)
    slot_index, slot_source = jax.vmap(functools.partial(slot_tables, experts=EXPERTS, capacity=CAP))(blocks)
    offsets = (jnp.arange(N_DP, dtype=jnp.int32) * count)[:, None]
    global_source = jnp.where(slot_source < count, slot_source + offsets, N_DP * count).astype(jnp.int32)
    by_expert = global_source.reshape(N_DP, EXPERTS, CAP).transpose(1, 0, 2).reshape(EXPERTS, N_DP * CAP)
    trunk_pad = jnp.concatenate([trunk, jnp.zeros((1, D), jnp.bfloat16)], axis=0)
    out_grad = jnp.einsum('rtk,trh->rkh', task_gates.astype(jnp.float32), mixture_grad.astype(jnp.float32)).astype(jnp.bfloat16)
    grad_pad = jnp.concatenate([out_grad.reshape(BATCH * TOP, H), jnp.zeros((1, H), jnp.bfloat16)], axis=0)

    def per_expert(packed):
        weight, source = packed
        expert_rows = trunk_pad[source // TOP]
        pre_act = jnp.dot(expert_rows, weight, preferred_element_type=jnp.float32)
        outputs = jax.nn.silu(pre_act).astype(jnp.bfloat16)
        slot_grad = grad_pad[source]
        pre_grad = (slot_grad.astype(jnp.float32) * silu_grad(pre_act)).astype(jnp.bfloat16)
        weight_grad = lax.dot_general(expert_rows, pre_grad, (((0,), (0,)), ((), ())), preferred_element_type=jnp.float32)
        return (outputs, weight_grad)
    outputs, expert_grad = lax.map(per_expert, (expert_weights, by_expert))
    place = slot_index - blocks * CAP
    flat_out = blocks * (N_DP * CAP) + (jnp.arange(N_DP, dtype=jnp.int32) * CAP)[:, None] + place
    picked = outputs.reshape(EXPERTS * N_DP * CAP, H)[flat_out.reshape(-1).astype(jnp.int32)].reshape(BATCH, TOP, H)
    mixture = lax.optimization_barrier(jnp.sum(task_gates[:, :, :, None] * picked[:, None, :, :].astype(jnp.float32), axis=2))
    task_mixture = jnp.transpose(mixture, (1, 0, 2)).astype(jnp.bfloat16)
    return (task_mixture, expert_grad)
```

```python
import math

import jax
import jax.numpy as jnp
from jax import lax
from jax.sharding import PartitionSpec as P

NEMB = 16
DEMB = 128
F32 = jnp.float32
BF16 = jnp.bfloat16


def silu_grad(pre_act):
    sigma = jax.nn.sigmoid(pre_act)
    return sigma + pre_act * sigma * (1.0 - sigma)


def slot_table(route, experts, capacity):
    rows = route.shape[0]
    lanes = jnp.arange(experts, dtype=jnp.int32)
    member = jnp.sum((route[:, :, None] == lanes).astype(F32), axis=1)
    earlier = (jnp.arange(rows)[:, None] > jnp.arange(rows)[None, :]).astype(BF16)
    prefix = jnp.dot(earlier, member.astype(BF16), preferred_element_type=F32).astype(jnp.int32)
    place = jnp.sum((route[:, :, None] == lanes) * prefix[:, None, :], axis=2)
    return route * capacity + place


def interaction(whole, gain):
    wide = whole.astype(F32)
    scale = lax.rsqrt(jnp.mean(wide * wide, axis=1, keepdims=True) + 1e-05)
    normed = (wide * scale * gain[None, :]).astype(BF16)
    cube = normed.reshape(normed.shape[0], NEMB, DEMB)
    gram = jnp.einsum("rnd,rmd->rnm", cube, cube, preferred_element_type=F32) / math.sqrt(DEMB)
    inter = jnp.einsum(
        "rnm,rmd->rnd", gram, cube.astype(F32), precision=lax.Precision.HIGHEST
    ) / math.sqrt(NEMB)
    return inter.reshape(whole.shape[0], NEMB * DEMB).astype(BF16)


def on_device(
    embeddings, trunk_weights, trunk_gains, expert_weights, route_ids, task_gates, mixture_grad
):
    trunk = embeddings
    for block_index in range(trunk_weights.shape[0]):
        whole = lax.all_gather(trunk, "tensor", axis=1, tiled=True)
        inter = interaction(whole, trunk_gains[block_index])
        branch = jax.nn.silu(
            jnp.dot(inter, trunk_weights[block_index], preferred_element_type=F32)
        )
        trunk = (trunk.astype(F32) + branch).astype(BF16)
    experts = lax.axis_size("tensor")
    local_rows, top_count = route_ids.shape
    capacity = 2 * local_rows * top_count // experts
    width = trunk.shape[1]
    slots = slot_table(route_ids, experts, capacity)
    all_slots = jnp.arange(experts * capacity, dtype=jnp.int32)
    hot = [(slots[:, k][None, :] == all_slots[:, None]).astype(BF16) for k in range(top_count)]
    outgoing = jnp.dot(sum(hot), trunk, preferred_element_type=F32).astype(BF16)
    expert_rows = lax.all_to_all(
        outgoing.reshape(experts, capacity, width), "tensor", split_axis=0, concat_axis=2, tiled=True
    )[0]
    wide_grad = mixture_grad.astype(F32)
    sent_grad = 0.0
    for k in range(top_count):
        out_grad = (
            task_gates[:, 0, k, None] * wide_grad[0] + task_gates[:, 1, k, None] * wide_grad[1]
        ).astype(BF16)
        sent_grad = sent_grad + jnp.dot(hot[k], out_grad, preferred_element_type=F32)
    slot_grad = lax.all_to_all(
        sent_grad.astype(BF16).reshape(experts, capacity, width),
        "tensor", split_axis=0, concat_axis=2, tiled=True,
    )[0]
    pre_act = jnp.dot(expert_rows, expert_weights[0], preferred_element_type=F32)
    outputs = jax.nn.silu(pre_act).astype(BF16)
    pre_grad = (slot_grad.astype(F32) * silu_grad(pre_act)).astype(BF16)
    local_grad = lax.dot_general(
        expert_rows, pre_grad, (((0,), (0,)), ((), ())), preferred_element_type=F32
    ).astype(BF16)
    weight_grad = lax.psum_scatter(local_grad, "dp", scatter_dimension=0, tiled=True).astype(F32)
    returned = lax.all_to_all(
        outputs.reshape(capacity, experts, width).transpose(1, 0, 2),
        "tensor", split_axis=0, concat_axis=0, tiled=True,
    ).reshape(experts * capacity, width)
    mixture = 0.0
    for k in range(top_count):
        picked = lax.dot_general(
            hot[k], returned, (((0,), (0,)), ((), ())), preferred_element_type=F32
        )
        mixture = mixture + task_gates[:, :, k].T[:, :, None] * picked[None]
    return (mixture.astype(BF16), weight_grad[None])


def solution(mesh):
    in_specs = (
        P("dp", "tensor"),
        P(None, None, "tensor"),
        P(),
        P("tensor", None, None),
        P("dp", None),
        P("dp", None, None),
        P(None, "dp", "tensor"),
    )
    out_specs = (P(None, "dp", "tensor"), P("tensor", "dp", None))
    return jax.shard_map(
        on_device, mesh=mesh, in_specs=in_specs, out_specs=out_specs, check_vma=False
    )
```

```python
import math

import jax
import jax.numpy as jnp
from jax import lax
from jax.experimental import pallas as pl
from jax.experimental.pallas import tpu as pltpu
from jax.sharding import PartitionSpec as P

NEMB = 16
DEMB = 128
GROUP = 16
CHUNKS = 4
F32 = jnp.float32
BF16 = jnp.bfloat16
MESH = pl.DeviceIdType.MESH


def slot_table(route, experts, capacity):
    rows = route.shape[0]
    lanes = jnp.arange(experts, dtype=jnp.int32)
    member = jnp.sum((route[:, :, None] == lanes).astype(F32), axis=1)
    earlier = (jnp.arange(rows)[:, None] > jnp.arange(rows)[None, :]).astype(BF16)
    prefix = jnp.dot(earlier, member.astype(BF16), preferred_element_type=F32).astype(jnp.int32)
    place = jnp.sum((route[:, :, None] == lanes) * prefix[:, None, :], axis=2)
    return route * capacity + place


def dot(a, b):
    return jnp.dot(a, b, preferred_element_type=F32)


def remote(src, dst, send_sem, recv_sem, axis, index):
    return pltpu.make_async_remote_copy(
        src_ref=src, dst_ref=dst, send_sem=send_sem, recv_sem=recv_sem,
        device_id={axis: index}, device_id_type=MESH,
    )


def greet(axis_peers):
    barrier = pltpu.get_barrier_semaphore()
    for axis, peer in axis_peers:
        pl.semaphore_signal(barrier, inc=1, device_id={axis: peer}, device_id_type=MESH)
    pl.semaphore_wait(barrier, len(axis_peers))


def trunk_kernel(
    emb, gains, weights, slot_rows, gates, grad, rows_out, grad_out,
    whole, nrm, inter, mask, cot, outg, send, recv, gsend, grecv,
):
    n_dev, rows, width = outg.shape[0], emb.shape[0], emb.shape[1]
    step_rows = rows // CHUNKS
    half = step_rows // 2
    cap = outg.shape[1]
    ring = n_dev // 2
    me = lax.axis_index("tensor")
    y, core = me // 2, me % 2
    right = ((y + 1) % ring) * 2 + core
    left = ((y + ring - 1) % ring) * 2 + core
    far = ((y + 2) % ring) * 2 + core
    sib = y * 2 + 1 - core

    def block(i, owner, lo=0, size=step_rows):
        return whole.at[i // CHUNKS, owner, pl.ds((i % CHUNKS) * step_rows + lo, size)]

    def copy(i, which):
        owner, lo, size, to = (
            (me, 0, step_rows, sib), (me, 0, step_rows, right), (me, 0, step_rows, left),
            (left, 0, step_rows, sib), (right, 0, step_rows, sib),
            (left, half, half, right), (right, 0, half, left),
            (far, half, half, sib), (far, 0, half, sib),
        )[which]
        ref = block(i, owner, lo, size)
        return remote(ref, ref, send.at[i, which], recv.at[i, which], "tensor", to)

    sib_left, sib_right = left + 1 - 2 * core, right + 1 - 2 * core
    sib_far = far + 1 - 2 * core

    def arrived(i, which):
        owner, lo, size = (
            (sib, 0, step_rows), (left, 0, step_rows), (right, 0, step_rows),
            (sib_left, 0, step_rows), (sib_right, 0, step_rows),
            (far, half, half), (far, 0, half),
            (sib_far, half, half), (sib_far, 0, half),
        )[which]
        ref = block(i, owner, lo, size)
        remote(ref, ref, send.at[i, which], recv.at[i, which], "tensor", sib).wait_recv()

    def begin(i):
        for which in (1, 2, 0):
            copy(i, which).start()

    def relay(i):
        arrived(i, 1)
        copy(i, 5).start()
        arrived(i, 2)
        copy(i, 6).start()
        copy(i, 3).start()
        copy(i, 4).start()

    def relay_far(i):
        arrived(i, 5)
        copy(i, 7).start()
        arrived(i, 6)
        copy(i, 8).start()

    def complete(i):
        for which in (0, 3, 4, 7, 8):
            arrived(i, which)

    whole[0, me] = emb[...]
    greet([("tensor", (me + d) % n_dev) for d in range(1, n_dev)])

    @pl.loop(0, CHUNKS)
    def _(i):
        begin(i)

    row_id = lax.broadcasted_iota(jnp.int32, mask.shape, 0) % GROUP
    col_id = lax.broadcasted_iota(jnp.int32, mask.shape, 1) % GROUP
    mask[...] = jnp.where(row_id == col_id, 1.0 / math.sqrt(DEMB * NEMB), 0.0)
    relay(0)
    for k in range(2):
        cot[k] = (
            gates[:, k : k + 1] * grad[0].astype(F32) + gates[:, 2 + k : 3 + k] * grad[1].astype(F32)
        ).astype(BF16)
    relay(1)
    relay_far(0)

    def chosen(expert, k):
        wanted = lax.broadcasted_iota(jnp.int32, (cap, rows), 0) + expert * cap
        return (slot_rows[k : k + 1, :] == wanted).astype(F32).astype(BF16)

    @pl.loop(0, n_dev)
    def _(e):
        outg[e] = (dot(chosen(e, 0), cot[0]) + dot(chosen(e, 1), cot[1])).astype(BF16)

    def grad_copy(d):
        to = (me + d) % n_dev
        return remote(outg.at[to], grad_out.at[me], gsend.at[d], grecv.at[d], "tensor", to)

    grad_out[me] = outg[me]

    @pl.loop(0, 2 * CHUNKS)
    def _(i):
        stage, first = i // CHUNKS, (i % CHUNKS) * step_rows
        span = pl.ds(first, step_rows)
        relay(i + 2)
        relay_far(i + 1)
        complete(i)

        def tile(n):
            return whole[stage, n // 2, span, (n % 2) * DEMB : (n % 2 + 1) * DEMB].astype(F32)

        total = jnp.zeros((step_rows, DEMB), F32)
        for n in range(NEMB):
            x = tile(n)
            total = total + x * x
        mean = jnp.sum(total, axis=1, keepdims=True) / (NEMB * DEMB)
        scale = lax.rsqrt(mean + 1e-05)
        for n in range(NEMB):
            gain = gains[stage, :, n * DEMB : (n + 1) * DEMB]
            nrm[n] = (tile(n) * scale * gain).astype(BF16)

        @pl.loop(0, step_rows // GROUP // 4)
        def _(g4):
            for g in range(4):
                at = pl.ds(pl.multiple_of((g4 * 4 + g) * GROUP, GROUP), GROUP)
                stack = nrm[:, at, :].reshape(NEMB * GROUP, DEMB)
                gram = lax.dot_general(
                    stack, stack, (((1,), (1,)), ((), ())), preferred_element_type=F32
                ) * mask[...]
                high = gram.astype(BF16)
                low = (gram - high.astype(F32)).astype(BF16)
                mixed = (dot(high, stack) + dot(low, stack)).astype(BF16)
                mixed = mixed.reshape(NEMB, GROUP, DEMB)
                for n in range(NEMB):
                    inter[at, n * DEMB : (n + 1) * DEMB] = mixed[n]

        pre = dot(inter[...], weights[stage])
        value = whole[stage, me, span].astype(F32) + pre * jax.nn.sigmoid(pre)
        whole[stage + 1, me, span] = value.astype(BF16)
        begin(i + CHUNKS)

        @pl.when(i < n_dev - 1)
        def _():
            grad_copy(i + 1).start()

    for i in range(2 * CHUNKS, 3 * CHUNKS):
        if i + 2 < 3 * CHUNKS:
            relay(i + 2)
        if i + 1 < 3 * CHUNKS:
            relay_far(i + 1)
        complete(i)

    mine = (chosen(me, 0).astype(F32) + chosen(me, 1).astype(F32)).astype(BF16)
    for q in range(n_dev):
        rows_out[:, q * width : (q + 1) * width] = dot(mine, whole[2, q]).astype(BF16)

    @pl.loop(0, 3 * CHUNKS)
    def _(i):
        for which in range(9):
            copy(i, which).wait_send()

    @pl.loop(1, n_dev)
    def _(d):
        grad_copy(d).wait_send()
        source = (me + n_dev - d) % n_dev
        remote(
            outg.at[me], grad_out.at[source], gsend.at[d], grecv.at[d], "tensor", source
        ).wait_recv()


def expert_kernel(
    rows_in, weight, slot_grad, slot_cols, gates, mix_out, wgrad_out,
    held_weight, rows_t, pgrad, outs, ret, first_buf, ring_buf, last_buf,
    wsem, send1, recv1, send2, recv2, osend, orecv,
):
    n_dev, cap, width = outs.shape
    part = pgrad.shape[1] // 4
    piece = wgrad_out.shape[0]
    me = lax.axis_index("tensor")
    dp = lax.axis_index("dp")
    cx, cz = dp // 4, dp % 4

    def load(h):
        span = pl.ds(h * part, part)
        return pltpu.make_async_copy(weight.at[:, span], held_weight.at[:, span], wsem.at[h])

    for h in range(4):
        load(h).start()

    def place(h, u, v):
        return u * 4 + v if h < 2 else v * 4 + u

    coord = [(cx, cz), (cx, cz), (cz, cx), (cz, cx)]
    sign = [1, 3, 1, 3]

    greet(
        [("dp", place(0, (cx + 1) % 4, cz)), ("dp", place(0, (cx + 3) % 4, cz)),
         ("dp", place(0, cx, (cz + 1) % 4)), ("dp", place(0, cx, (cz + 3) % 4))]
        + [("tensor", (me + d) % n_dev) for d in range(1, n_dev)]
    )

    eye = (
        lax.broadcasted_iota(jnp.int32, (width, width), 0)
        == lax.broadcasted_iota(jnp.int32, (width, width), 1)
    ).astype(F32).astype(BF16)
    for q in range(n_dev):
        rows_t[q * width : (q + 1) * width, :] = lax.dot_general(
            eye, rows_in[:, q * width : (q + 1) * width], (((1,), (1,)), ((), ())),
            preferred_element_type=F32,
        ).astype(BF16)

    def partial(h, t, j):
        u, v = coord[h]
        owner = place(h, (u + (4 - sign[h]) * (1 + t)) % 4, (v + (4 - sign[h]) * (1 + j)) % 4)
        at = pl.ds(pl.multiple_of(owner * piece, piece), piece)
        return dot(rows_t[at, :], pgrad[:, h * part : (h + 1) * part])

    def hop1(h, k, src):
        u, v = coord[h]
        return remote(
            src, ring_buf.at[h, k], send1.at[h, k], recv1.at[h, k],
            "dp", place(h, (u + sign[h]) % 4, v),
        )

    def hop2(h, j):
        u, v = coord[h]
        return remote(
            ring_buf.at[h, 8 + j], last_buf.at[h, j], send2.at[h, j], recv2.at[h, j],
            "dp", place(h, u, (v + sign[h]) % 4),
        )

    for h in range(4):
        load(h).wait()
        for p in range(2 * h, 2 * h + 2):
            cols = slice(p * width, (p + 1) * width)
            pre = dot(rows_in[...], held_weight[:, cols])
            sigma = jax.nn.sigmoid(pre)
            outs[p] = (pre * sigma).astype(BF16)
            slope = sigma + pre * sigma * (1.0 - sigma)
            pgrad[:, cols] = (slot_grad[p].astype(F32) * slope).astype(BF16)

        @pl.loop(0, 4)
        def _(j):
            first_buf[h, j] = partial(h, 0, j).astype(BF16)
            hop1(h, j, first_buf.at[h, j]).start()

    def out_copy(d):
        to = (me + d) % n_dev
        return remote(outs.at[to], ret.at[me], osend.at[d], orecv.at[d], "tensor", to)

    @pl.loop(1, n_dev)
    def _(d):
        out_copy(d).start()

    ret[me] = outs[me]

    def ring_step(k):
        t, j = k // 4, k % 4
        for h in range(4):
            own = partial(h, t, j)
            hop1(h, k - 4, ring_buf.at[h, k - 4]).wait_recv()
            ring_buf[h, k - 4] = (ring_buf[h, k - 4].astype(F32) + own).astype(BF16)
            hop1(h, k, ring_buf.at[h, k - 4]).start()

    pl.loop(4, 8)(ring_step)

    @pl.loop(1, n_dev)
    def _(d):
        source = (me + n_dev - d) % n_dev
        remote(
            outs.at[me], ret.at[source], osend.at[d], orecv.at[d], "tensor", source
        ).wait_recv()

    block_rows = 128

    @pl.loop(0, mix_out.shape[1] // block_rows)
    def _(b):
        at = pl.ds(pl.multiple_of(b * block_rows, block_rows), block_rows)
        lane = lax.broadcasted_iota(jnp.int32, (block_rows, cap), 1)
        picked = []
        for k in range(2):
            slot = slot_cols[at, k : k + 1]
            total = jnp.zeros((block_rows, width), F32)
            for e in range(n_dev):
                hot = (slot == lane + e * cap).astype(F32).astype(BF16)
                total = total + dot(hot, ret[e])
            picked.append(total)
        for t in range(2):
            mix = (
                gates[at, 2 * t : 2 * t + 1] * picked[0]
                + gates[at, 2 * t + 1 : 2 * t + 2] * picked[1]
            )
            mix_out[t, at, :] = mix.astype(BF16)

    pl.loop(8, 12)(ring_step)

    for j in range(4):
        for h in range(4):
            own = partial(h, 3, j)
            hop1(h, 8 + j, ring_buf.at[h, 8 + j]).wait_recv()
            total = ring_buf[h, 8 + j].astype(F32) + own
            if j > 0:
                hop2(h, j - 1).wait_recv()
                total = total + last_buf[h, j - 1].astype(F32)
            if j < 3:
                ring_buf[h, 8 + j] = total.astype(BF16)
                hop2(h, j).start()
            else:
                wgrad_out[:, h * part : (h + 1) * part] = total

    for h in range(4):
        @pl.loop(0, 4)
        def _(k):
            hop1(h, k, first_buf.at[h, k]).wait_send()

        @pl.loop(4, 12)
        def _(k):
            hop1(h, k, ring_buf.at[h, k - 4]).wait_send()

        for j in range(3):
            hop2(h, j).wait_send()

    @pl.loop(1, n_dev)
    def _(d):
        out_copy(d).wait_send()


VMEM = pl.BlockSpec(memory_space=pltpu.VMEM)
DMA = pltpu.SemaphoreType.DMA


def on_device(
    embeddings, trunk_weights, trunk_gains, expert_weights, route_ids, task_gates, mixture_grad
):
    experts = lax.axis_size("tensor")
    rows, top = route_ids.shape
    cap = 2 * rows * top // experts
    width = embeddings.shape[1]
    full = width * experts
    slots = slot_table(route_ids, experts, cap)
    gates = task_gates.reshape(rows, -1)
    step_rows = rows // CHUNKS

    expert_rows, slot_grad = pl.pallas_call(
        trunk_kernel,
        out_shape=(
            jax.ShapeDtypeStruct((cap, full), BF16),
            jax.ShapeDtypeStruct((experts, cap, width), BF16),
        ),
        in_specs=[VMEM] * 6,
        out_specs=(VMEM, VMEM),
        scratch_shapes=[
            pltpu.VMEM((3, experts, rows, width), BF16),
            pltpu.VMEM((NEMB, step_rows, DEMB), BF16),
            pltpu.VMEM((step_rows, full), BF16),
            pltpu.VMEM((NEMB * GROUP, NEMB * GROUP), F32),
            pltpu.VMEM((2, rows, width), BF16),
            pltpu.VMEM((experts, cap, width), BF16),
            DMA((3 * CHUNKS, 9)),
            DMA((3 * CHUNKS, 9)),
            DMA((experts,)),
            DMA((experts,)),
        ],
        compiler_params=pltpu.CompilerParams(
            collective_id=0, has_side_effects=True, vmem_limit_bytes=40 << 20
        ),
        cost_estimate=pl.CostEstimate(flops=6 << 30, bytes_accessed=8 << 20, transcendentals=0),
        name="trunk",
    )(embeddings, trunk_gains[:, None, :], trunk_weights, slots.T, gates, mixture_grad)

    piece = full // lax.axis_size("dp")
    part = full // 4
    mixture, weight_grad = pl.pallas_call(
        expert_kernel,
        out_shape=(
            jax.ShapeDtypeStruct((2, rows, width), BF16),
            jax.ShapeDtypeStruct((piece, full), F32),
        ),
        in_specs=[VMEM, pl.BlockSpec(memory_space=pl.ANY), VMEM, VMEM, VMEM],
        out_specs=(VMEM, VMEM),
        scratch_shapes=[
            pltpu.VMEM((full, full), BF16),
            pltpu.VMEM((full, cap), BF16),
            pltpu.VMEM((cap, full), BF16),
            pltpu.VMEM((experts, cap, width), BF16),
            pltpu.VMEM((experts, cap, width), BF16),
            pltpu.VMEM((4, 4, piece, part), BF16),
            pltpu.VMEM((4, 12, piece, part), BF16),
            pltpu.VMEM((4, 3, piece, part), BF16),
            DMA((4,)),
            DMA((4, 12)),
            DMA((4, 12)),
            DMA((4, 3)),
            DMA((4, 3)),
            DMA((experts,)),
            DMA((experts,)),
        ],
        compiler_params=pltpu.CompilerParams(
            collective_id=1, has_side_effects=True, vmem_limit_bytes=48 << 20
        ),
        cost_estimate=pl.CostEstimate(flops=6 << 30, bytes_accessed=12 << 20, transcendentals=0),
        name="experts",
    )(expert_rows, expert_weights[0], slot_grad, slots, gates)
    return (mixture, weight_grad[None])


def solution(mesh):
    in_specs = (
        P("dp", "tensor"),
        P(None, None, "tensor"),
        P(),
        P("tensor", None, None),
        P("dp", None),
        P("dp", None, None),
        P(None, "dp", "tensor"),
    )
    out_specs = (P(None, "dp", "tensor"), P("tensor", "dp", None))
    return jax.shard_map(
        on_device, mesh=mesh, in_specs=in_specs, out_specs=out_specs, check_vma=False
    )
```

```python
import math

import jax
import jax.numpy as jnp
from jax import lax
from jax.experimental import pallas as pl
from jax.experimental.pallas import tpu as pltpu
from jax.sharding import PartitionSpec as P

NEMB = 16
DEMB = 128
GROUP = 16
CHUNKS = 4
RELAY = 2
FAR = 1
F32 = jnp.float32
BF16 = jnp.bfloat16
MESH = pl.DeviceIdType.MESH


def dot(a, b):
    return jnp.dot(a, b, preferred_element_type=F32)


def dot_nt(a, b):
    return lax.dot_general(a, b, (((1,), (1,)), ((), ())), preferred_element_type=F32)


def remote(src, dst, send_sem, recv_sem, axis, index):
    return pltpu.make_async_remote_copy(
        src_ref=src, dst_ref=dst, send_sem=send_sem, recv_sem=recv_sem,
        device_id={axis: index}, device_id_type=MESH,
    )


def greet(axis_peers):
    barrier = pltpu.get_barrier_semaphore()
    for axis, peer in axis_peers:
        pl.semaphore_signal(barrier, inc=1, device_id={axis: peer}, device_id_type=MESH)
    pl.semaphore_wait(barrier, len(axis_peers))


def kernel(
    emb, gains, weights, experts_in, ids, gates_in, grad_in, mix_out, wgrad_out,
    whole, nrm, inter, mask, wheld, grad, cot, outg, slot_grad, table, cols,
    held, rows_in, rows_t, slopes, pgrad, outs, ret, first_buf, ring_buf, last_buf,
    lsem, wsem, send, recv, gsend, grecv, send1, recv1, send2, recv2, osend, orecv,
):
    n_dev, cap, width = outs.shape
    rows = emb.shape[0]
    piece, part = first_buf.shape[2:]
    items, live = 3 * CHUNKS, 2 * CHUNKS
    step_rows = rows // CHUNKS
    ring = n_dev // 2
    me = lax.axis_index("tensor")
    dp = lax.axis_index("dp")
    cx, cz = dp // 4, dp % 4
    y, core = me // 2, me % 2
    right = ((y + 1) % ring) * 2 + core
    left = ((y + ring - 1) % ring) * 2 + core
    far = ((y + 2) % ring) * 2 + core
    flip = 1 - 2 * core
    sib = me + flip

    load_emb = pltpu.make_async_copy(emb, whole.at[0, me], lsem.at[0])
    load_grad = pltpu.make_async_copy(grad_in, grad, lsem.at[1])
    load_weights = pltpu.make_async_copy(weights, wheld, lsem.at[2])

    def load_expert(h):
        span = pl.ds(h * 2 * width, 2 * width)
        return pltpu.make_async_copy(experts_in.at[:, span], held.at[:, span], wsem.at[h])

    load_emb.start()
    load_grad.start()
    load_weights.start()

    def copy(i, which):
        turn = (i % 2) * (right - left)
        owner, to = (
            (me, sib), (me, right), (me, left), (left, sib), (right, sib),
            (left + turn, right - turn), (far, sib),
        )[which]
        at = pl.ds((i % CHUNKS) * step_rows, step_rows)
        ref = whole.at[i // CHUNKS, owner, at]
        return remote(ref, ref, send.at[i, which], recv.at[i, which], "tensor", to)

    def arrived(i, which):
        owner = (sib, left, right, left + flip, right + flip, far, far + flip)[which]
        at = pl.ds((i % CHUNKS) * step_rows, step_rows)
        ref = whole.at[i // CHUNKS, owner, at]
        remote(ref, ref, send.at[i, which], recv.at[i, which], "tensor", sib).wait_recv()

    def begin(i):
        for which in (1, 2, 0):
            copy(i, which).start()

    def relay(i):
        arrived(i, 1)
        arrived(i, 2)
        for which in (5, 3, 4):
            copy(i, which).start()

    def relay_far(i):
        arrived(i, 5)
        copy(i, 6).start()

    def complete(i):
        for which in (0, 3, 4, 6):
            arrived(i, which)

    def place(h, u, v):
        return u * 4 + v if h < 2 else v * 4 + u

    coord = [(cx, cz), (cx, cz), (cz, cx), (cz, cx)]
    sign = [1, 3, 1, 3]

    load_emb.wait()
    greet(
        [("tensor", (me + d) % n_dev) for d in range(1, n_dev)]
        + [("dp", place(0, (cx + 1) % 4, cz)), ("dp", place(0, (cx + 3) % 4, cz)),
           ("dp", place(0, cx, (cz + 1) % 4)), ("dp", place(0, cx, (cz + 3) % 4))]
    )

    @pl.loop(0, CHUNKS)
    def _(i):
        begin(i)

    for h in range(4):
        load_expert(h).start()

    row_id = lax.broadcasted_iota(jnp.int32, mask.shape, 0) % GROUP
    col_id = lax.broadcasted_iota(jnp.int32, mask.shape, 1) % GROUP
    mask[...] = jnp.where(row_id == col_id, 1.0 / math.sqrt(DEMB * NEMB), 0.0)

    lane = lax.broadcasted_iota(jnp.int32, (n_dev, rows), 0)
    is_first = (ids[0:1, :] == lane).astype(F32)
    is_second = (ids[1:2, :] == lane).astype(F32)
    member = (is_first + is_second).astype(BF16)
    earlier = (
        lax.broadcasted_iota(jnp.int32, (rows, rows), 0)
        < lax.broadcasted_iota(jnp.int32, (rows, rows), 1)
    ).astype(F32).astype(BF16)
    slot_of = dot(member, earlier) + lane.astype(F32) * cap
    table[...] = jnp.zeros(table.shape, F32)
    table[0:1, :] = jnp.sum(is_first * slot_of, axis=0, keepdims=True)
    table[1:2, :] = jnp.sum(is_second * slot_of, axis=0, keepdims=True)
    for t in range(2):
        table[2 + 2 * t : 4 + 2 * t, :] = gates_in[t]
    cols[...] = table[...].T

    def gate(at, t, k):
        return cols[at, 2 + 2 * t + k : 3 + 2 * t + k]

    def chosen(expert, k):
        wanted = lax.broadcasted_iota(jnp.int32, (cap, rows), 0) + expert * cap
        return (table[k : k + 1, :].astype(jnp.int32) == wanted).astype(F32).astype(BF16)

    load_grad.wait()
    every = slice(0, rows)
    for k in range(2):
        cot[k] = (
            gate(every, 0, k) * grad[0].astype(F32) + gate(every, 1, k) * grad[1].astype(F32)
        ).astype(BF16)

    def cotangent(e):
        outg[e] = (dot(chosen(e, 0), cot[0]) + dot(chosen(e, 1), cot[1])).astype(BF16)

    for e in range(4):
        cotangent(e)
    for i in range(RELAY):
        relay(i)
        if 0 < i <= FAR:
            relay_far(i - 1)
    load_weights.wait()

    @pl.loop(0, live)
    def _(i):
        stage, first = i // CHUNKS, (i % CHUNKS) * step_rows
        span = pl.ds(pl.multiple_of(first, step_rows), step_rows)
        complete(i)

        def tile(n):
            return whole[stage, n // 2, span, (n % 2) * DEMB : (n % 2 + 1) * DEMB].astype(F32)

        total = jnp.zeros((step_rows, DEMB), F32)
        for n in range(NEMB):
            x = tile(n)
            total = total + x * x
        mean = jnp.sum(total, axis=1, keepdims=True) / (NEMB * DEMB)
        scale = lax.rsqrt(mean + 1e-05)
        for n in range(NEMB):
            lanes = slice(n * DEMB, (n + 1) * DEMB)
            gain = jnp.where(stage == 0, gains[0:1, lanes], gains[1:2, lanes])
            nrm[n] = (tile(n) * scale * gain).astype(BF16)
        relay(i + RELAY)
        relay_far(i + FAR)

        @pl.loop(0, step_rows // GROUP // 4)
        def _(g4):
            for g in range(4):
                at = pl.ds(pl.multiple_of((g4 * 4 + g) * GROUP, GROUP), GROUP)
                stack = nrm[:, at, :].reshape(NEMB * GROUP, DEMB)
                gram = dot_nt(stack, stack) * mask[...]
                high = gram.astype(BF16)
                low = (gram - high.astype(F32)).astype(BF16)
                mixed = (dot(high, stack) + dot(low, stack)).astype(BF16)
                mixed = mixed.reshape(NEMB, GROUP, DEMB)
                for n in range(NEMB):
                    inter[at, n * DEMB : (n + 1) * DEMB] = mixed[n]

        pre = dot(inter[...], wheld[stage])
        value = whole[stage, me, span].astype(F32) + pre * jax.nn.sigmoid(pre)
        whole[stage + 1, me, span] = value.astype(BF16)
        begin(i + CHUNKS)

    def to_expert(d):
        to = (me + d) % n_dev
        return remote(outg.at[to], slot_grad.at[me], gsend.at[d], grecv.at[d], "tensor", to)

    for i in range(live, items):
        if i + RELAY < items:
            relay(i + RELAY)
        if i + FAR < items:
            relay_far(i + FAR)
        if i < live + 2:
            for e in range(4 + 2 * (i - live), 6 + 2 * (i - live)):
                cotangent(e)
        if i == items - 1 - FAR:
            @pl.loop(1, n_dev)
            def _(d):
                to_expert(d).start()
        complete(i)
    slot_grad[me] = outg[me]

    mine = (chosen(me, 0).astype(F32) + chosen(me, 1).astype(F32)).astype(BF16)
    for q in range(n_dev):
        rows_in[:, q * width : (q + 1) * width] = dot(mine, whole[2, q]).astype(BF16)
    eye = (
        lax.broadcasted_iota(jnp.int32, (width, width), 0)
        == lax.broadcasted_iota(jnp.int32, (width, width), 1)
    ).astype(F32).astype(BF16)
    for q in range(n_dev):
        rows_t[q * width : (q + 1) * width, :] = dot_nt(
            eye, rows_in[:, q * width : (q + 1) * width]
        ).astype(BF16)

    def partial(h, t, j):
        u, v = coord[h]
        owner = place(h, (u + (4 - sign[h]) * (1 + t)) % 4, (v + (4 - sign[h]) * (1 + j)) % 4)
        at = pl.ds(pl.multiple_of(owner * piece, piece), piece)
        return dot(rows_t[at, :], pgrad[:, h * part : (h + 1) * part])

    def hop1(h, k, src):
        u, v = coord[h]
        return remote(
            src, ring_buf.at[h, k], send1.at[h, k], recv1.at[h, k],
            "dp", place(h, (u + sign[h]) % 4, v),
        )

    def hop2(h, j):
        u, v = coord[h]
        return remote(
            ring_buf.at[h, 8 + j], last_buf.at[h, j],
            send2.at[h, j], recv2.at[h, j], "dp", place(h, u, (v + sign[h]) % 4),
        )

    for p in range(n_dev):
        if p % 2 == 0:
            load_expert(p // 2).wait()
        pre = dot(rows_in[...], held[:, p * width : (p + 1) * width])
        sigma = jax.nn.sigmoid(pre)
        outs[p] = (pre * sigma).astype(BF16)
        slopes[p] = sigma + pre * sigma * (1.0 - sigma)

    @pl.loop(1, n_dev)
    def _(d):
        source = (me + n_dev - d) % n_dev
        remote(
            outg.at[me], slot_grad.at[source], gsend.at[d], grecv.at[d], "tensor", source
        ).wait_recv()

    for h in range(4):
        for p in range(2 * h, 2 * h + 2):
            pgrad[:, p * width : (p + 1) * width] = (
                slot_grad[p].astype(F32) * slopes[p]
            ).astype(BF16)

        @pl.loop(0, 4)
        def _(j):
            first_buf[h, j] = partial(h, 0, j).astype(BF16)
            hop1(h, j, first_buf.at[h, j]).start()

    def out_copy(d):
        to = (me + d) % n_dev
        return remote(outs.at[to], ret.at[me], osend.at[d], orecv.at[d], "tensor", to)

    @pl.loop(1, n_dev)
    def _(d):
        out_copy(d).start()

    ret[me] = outs[me]

    def ring_step(k):
        t, j = k // 4, k % 4
        own = [partial(h, t, j) for h in range(4)]
        for h in range(4):
            hop1(h, k - 4, ring_buf.at[h, k - 4]).wait_recv()
            ring_buf[h, k - 4] = (ring_buf[h, k - 4].astype(F32) + own[h]).astype(BF16)
            hop1(h, k, ring_buf.at[h, k - 4]).start()

    pl.loop(4, 8)(ring_step)

    @pl.loop(1, n_dev)
    def _(d):
        source = (me + n_dev - d) % n_dev
        remote(
            outs.at[me], ret.at[source], osend.at[d], orecv.at[d], "tensor", source
        ).wait_recv()

    block_rows = 128

    @pl.loop(0, rows // block_rows)
    def _(b):
        at = pl.ds(pl.multiple_of(b * block_rows, block_rows), block_rows)
        seat = lax.broadcasted_iota(jnp.int32, (block_rows, cap), 1)
        picked = []
        for k in range(2):
            slot = cols[at, k : k + 1].astype(jnp.int32)
            total = jnp.zeros((block_rows, width), F32)
            for e in range(n_dev):
                hot = (slot == seat + e * cap).astype(F32).astype(BF16)
                total = total + dot(hot, ret[e])
            picked.append(total)
        for t in range(2):
            mix = gate(at, t, 0) * picked[0] + gate(at, t, 1) * picked[1]
            mix_out[t, at, :] = mix.astype(BF16)

    pl.loop(8, 12)(ring_step)

    for j in range(4):
        for h in range(4):
            own = partial(h, 3, j)
            hop1(h, 8 + j, ring_buf.at[h, 8 + j]).wait_recv()
            total = ring_buf[h, 8 + j].astype(F32) + own
            if j > 0:
                hop2(h, j - 1).wait_recv()
                total = total + last_buf[h, j - 1].astype(F32)
            if j < 3:
                ring_buf[h, 8 + j] = total.astype(BF16)
                hop2(h, j).start()
            else:
                wgrad_out[:, h * part : (h + 1) * part] = total

    @pl.loop(0, items)
    def _(i):
        for which in range(7):
            copy(i, which).wait_send()

    for h in range(4):
        @pl.loop(0, 4)
        def _(k):
            hop1(h, k, first_buf.at[h, k]).wait_send()

        @pl.loop(4, 12)
        def _(k):
            hop1(h, k, ring_buf.at[h, k - 4]).wait_send()

        for j in range(3):
            hop2(h, j).wait_send()

    @pl.loop(1, n_dev)
    def _(d):
        to_expert(d).wait_send()
        out_copy(d).wait_send()


VMEM = pl.BlockSpec(memory_space=pltpu.VMEM)
ANY = pl.BlockSpec(memory_space=pl.ANY)
DMA = pltpu.SemaphoreType.DMA


def on_device(
    embeddings, trunk_weights, trunk_gains, expert_weights, route_ids, task_gates, mixture_grad
):
    experts = lax.axis_size("tensor")
    rows, top = route_ids.shape
    cap = 2 * rows * top // experts
    width = embeddings.shape[1]
    full = width * experts
    step_rows = rows // CHUNKS
    piece = full // lax.axis_size("dp")
    by_slot = (experts, cap, width)

    mixture, weight_grad = pl.pallas_call(
        kernel,
        out_shape=(
            jax.ShapeDtypeStruct((2, rows, width), BF16),
            jax.ShapeDtypeStruct((piece, full), F32),
        ),
        in_specs=[ANY, VMEM, ANY, ANY, VMEM, VMEM, ANY],
        out_specs=(VMEM, VMEM),
        scratch_shapes=[
            pltpu.VMEM((3, experts, rows, width), BF16),
            pltpu.VMEM((NEMB, step_rows, DEMB), BF16),
            pltpu.VMEM((step_rows, full), BF16),
            pltpu.VMEM((NEMB * GROUP, NEMB * GROUP), F32),
            pltpu.VMEM((2, full, width), BF16),
            pltpu.VMEM((2, rows, width), BF16),
            pltpu.VMEM((2, rows, width), BF16),
            pltpu.VMEM(by_slot, BF16),
            pltpu.VMEM(by_slot, BF16),
            pltpu.VMEM((128, rows), F32),
            pltpu.VMEM((rows, 128), F32),
            pltpu.VMEM((full, full), BF16),
            pltpu.VMEM((cap, full), BF16),
            pltpu.VMEM((full, cap), BF16),
            pltpu.VMEM(by_slot, F32),
            pltpu.VMEM((cap, full), BF16),
            pltpu.VMEM(by_slot, BF16),
            pltpu.VMEM(by_slot, BF16),
            pltpu.VMEM((4, 4, piece, full // 4), BF16),
            pltpu.VMEM((4, 12, piece, full // 4), BF16),
            pltpu.VMEM((4, 3, piece, full // 4), BF16),
            DMA((3,)),
            DMA((4,)),
            DMA((3 * CHUNKS, 7)),
            DMA((3 * CHUNKS, 7)),
            DMA((experts,)),
            DMA((experts,)),
            DMA((4, 12)),
            DMA((4, 12)),
            DMA((4, 3)),
            DMA((4, 3)),
            DMA((experts,)),
            DMA((experts,)),
        ],
        compiler_params=pltpu.CompilerParams(
            collective_id=0, has_side_effects=True, vmem_limit_bytes=56 << 20
        ),
        cost_estimate=pl.CostEstimate(flops=12 << 30, bytes_accessed=16 << 20, transcendentals=0),
        name="trunk_experts",
    )(
        embeddings, trunk_gains, trunk_weights, expert_weights[0], route_ids.T,
        task_gates.transpose(1, 2, 0), mixture_grad,
    )
    return (mixture, weight_grad[None])


def solution(mesh):
    in_specs = (
        P("dp", "tensor"),
        P(None, None, "tensor"),
        P(),
        P("tensor", None, None),
        P("dp", None),
        P("dp", None, None),
        P(None, "dp", "tensor"),
    )
    out_specs = (P(None, "dp", "tensor"), P("tensor", "dp", None))
    return jax.shard_map(
        on_device, mesh=mesh, in_specs=in_specs, out_specs=out_specs, check_vma=False
    )
```

```python
import math

import jax
import jax.numpy as jnp
from jax import lax
from jax.experimental import pallas as pl
from jax.experimental.pallas import tpu as pltpu
from jax.sharding import PartitionSpec as P

NEMB = 16
DEMB = 128
GROUP = 16
CHUNKS = 4
RELAY = 2
FAR = 1
F32 = jnp.float32
BF16 = jnp.bfloat16
MESH = pl.DeviceIdType.MESH


def dot(a, b):
    return jnp.dot(a, b, preferred_element_type=F32)


def dot_nt(a, b):
    return lax.dot_general(a, b, (((1,), (1,)), ((), ())), preferred_element_type=F32)


def remote(src, dst, send_sem, recv_sem, axis, index):
    return pltpu.make_async_remote_copy(
        src_ref=src, dst_ref=dst, send_sem=send_sem, recv_sem=recv_sem,
        device_id={axis: index}, device_id_type=MESH,
    )


def kernel(
    emb, gains_in, weights, experts_in, ids_in, gates_in, grad_in, mix_out, wgrad_out,
    whole, nrm, inter, mask, wheld, grad, gains, ids, gates, cot, outg, slot_grad, table, cols,
    held, rows_in, rows_t, slopes, pgrad, outs, ret, first_buf, ring_buf, last_buf,
    mix, wgrad, lsem, wsem, send, recv, gsend, grecv, send1, recv1, send2, recv2, osend, orecv, send0, recv0,
):
    n_dev, cap, width = outs.shape
    rows = emb.shape[0]
    piece, part = last_buf.shape[2:]
    items, live = 3 * CHUNKS, 2 * CHUNKS
    step_rows = rows // CHUNKS
    ring = n_dev // 2
    me = lax.axis_index("tensor")
    dp = lax.axis_index("dp")
    cx, cz = dp // 4, dp % 4
    y, core = me // 2, me % 2
    right = ((y + 1) % ring) * 2 + core
    left = ((y + ring - 1) % ring) * 2 + core
    far = ((y + 2) % ring) * 2 + core
    flip = 1 - 2 * core
    sib = me + flip

    load_emb = pltpu.make_async_copy(emb, whole.at[0, me], lsem.at[0])
    load_grad = pltpu.make_async_copy(grad_in, grad, lsem.at[1])
    load_weights = pltpu.make_async_copy(weights, wheld, lsem.at[2])
    load_gains = pltpu.make_async_copy(gains_in, gains, lsem.at[3])
    load_ids = pltpu.make_async_copy(ids_in, ids, lsem.at[4])
    load_gates = pltpu.make_async_copy(gates_in, gates, lsem.at[5])

    def load_expert(h):
        span = pl.ds(h * 2 * width, 2 * width)
        return pltpu.make_async_copy(experts_in.at[:, span], held.at[:, span], wsem.at[h])

    load_emb.start()
    for load in (load_ids, load_gates, load_gains, load_grad, load_weights):
        load.start()

    def place(h, u, v):
        return u * 4 + v if h < 2 else v * 4 + u

    barrier = pltpu.get_barrier_semaphore()
    peers = [("tensor", (me + d) % n_dev) for d in range(1, n_dev)] + [
        ("dp", place(0, (cx + 1) % 4, cz)), ("dp", place(0, (cx + 3) % 4, cz)),
        ("dp", place(0, cx, (cz + 1) % 4)), ("dp", place(0, cx, (cz + 3) % 4)),
    ]
    for axis, peer in peers:
        pl.semaphore_signal(barrier, inc=1, device_id={axis: peer}, device_id_type=MESH)

    def copy(i, which):
        turn = (i % 2) * (right - left)
        owner, to = (
            (me, sib), (me, right), (me, left), (left, sib), (right, sib),
            (left + turn, right - turn), (far, sib),
        )[which]
        at = pl.ds((i % CHUNKS) * step_rows, step_rows)
        ref = whole.at[i // CHUNKS, owner, at]
        return remote(ref, ref, send.at[i, which], recv.at[i, which], "tensor", to)

    def arrived(i, which):
        owner = (sib, left, right, left + flip, right + flip, far, far + flip)[which]
        at = pl.ds((i % CHUNKS) * step_rows, step_rows)
        ref = whole.at[i // CHUNKS, owner, at]
        remote(ref, ref, send.at[i, which], recv.at[i, which], "tensor", sib).wait_recv()

    def begin(i):
        for which in (1, 2, 0):
            copy(i, which).start()

    def relay(i):
        arrived(i, 1)
        arrived(i, 2)
        for which in (5, 3, 4):
            copy(i, which).start()

    def relay_far(i):
        arrived(i, 5)
        copy(i, 6).start()

    def complete(i):
        for which in (0, 3, 4, 6):
            arrived(i, which)

    coord = [(cx, cz), (cx, cz), (cz, cx), (cz, cx)]
    sign = [1, 3, 1, 3]

    load_emb.wait()
    pl.semaphore_wait(barrier, len(peers))

    @pl.loop(0, CHUNKS)
    def _(i):
        begin(i)

    for h in range(4):
        load_expert(h).start()

    row_id = lax.broadcasted_iota(jnp.int32, mask.shape, 0) % GROUP
    col_id = lax.broadcasted_iota(jnp.int32, mask.shape, 1) % GROUP
    mask[...] = jnp.where(row_id == col_id, 1.0 / math.sqrt(DEMB * NEMB), 0.0)

    load_ids.wait()
    load_gates.wait()
    lane = lax.broadcasted_iota(jnp.int32, (n_dev, rows), 0)
    is_first = (ids[0:1, :] == lane).astype(F32)
    is_second = (ids[1:2, :] == lane).astype(F32)
    member = (is_first + is_second).astype(BF16)
    earlier = (
        lax.broadcasted_iota(jnp.int32, (rows, rows), 0)
        < lax.broadcasted_iota(jnp.int32, (rows, rows), 1)
    ).astype(F32).astype(BF16)
    slot_of = dot(member, earlier) + lane.astype(F32) * cap
    table[...] = jnp.zeros(table.shape, F32)
    table[0:1, :] = jnp.sum(is_first * slot_of, axis=0, keepdims=True)
    table[1:2, :] = jnp.sum(is_second * slot_of, axis=0, keepdims=True)
    for t in range(2):
        table[2 + 2 * t : 4 + 2 * t, :] = gates[t]
    cols[...] = table[...].T

    def gate(at, t, k):
        return cols[at, 2 + 2 * t + k : 3 + 2 * t + k]

    def chosen(expert, k):
        wanted = lax.broadcasted_iota(jnp.int32, (cap, rows), 0) + expert * cap
        return (table[k : k + 1, :].astype(jnp.int32) == wanted).astype(F32).astype(BF16)

    load_grad.wait()
    every = slice(0, rows)
    for k in range(2):
        cot[k] = (
            gate(every, 0, k) * grad[0].astype(F32) + gate(every, 1, k) * grad[1].astype(F32)
        ).astype(BF16)

    def cotangent(e):
        outg[e] = (dot(chosen(e, 0), cot[0]) + dot(chosen(e, 1), cot[1])).astype(BF16)

    for e in range(4):
        cotangent(e)
    for i in range(RELAY):
        relay(i)
        if 0 < i <= FAR:
            relay_far(i - 1)
    load_gains.wait()
    load_weights.wait()

    @pl.loop(0, live)
    def _(i):
        stage, first = i // CHUNKS, (i % CHUNKS) * step_rows
        span = pl.ds(pl.multiple_of(first, step_rows), step_rows)
        complete(i)

        def tile(n):
            return whole[stage, n // 2, span, (n % 2) * DEMB : (n % 2 + 1) * DEMB].astype(F32)

        total = jnp.zeros((step_rows, DEMB), F32)
        for n in range(NEMB):
            x = tile(n)
            total = total + x * x
        mean = jnp.sum(total, axis=1, keepdims=True) / (NEMB * DEMB)
        scale = lax.rsqrt(mean + 1e-05)
        for n in range(NEMB):
            lanes = slice(n * DEMB, (n + 1) * DEMB)
            gain = jnp.where(stage == 0, gains[0:1, lanes], gains[1:2, lanes])
            nrm[n] = (tile(n) * scale * gain).astype(BF16)
        relay(i + RELAY)
        passes = step_rows // GROUP // 4

        @pl.loop(0, passes)
        def _(g4):
            @pl.when(g4 == passes // 2)
            def _():
                relay_far(i + FAR)

            for g in range(4):
                at = pl.ds(pl.multiple_of((g4 * 4 + g) * GROUP, GROUP), GROUP)
                stack = nrm[:, at, :].reshape(NEMB * GROUP, DEMB)
                gram = dot_nt(stack, stack) * mask[...]
                high = gram.astype(BF16)
                low = (gram - high.astype(F32)).astype(BF16)
                mixed = (dot(high, stack) + dot(low, stack)).astype(BF16)
                mixed = mixed.reshape(NEMB, GROUP, DEMB)
                for n in range(NEMB):
                    inter[at, n * DEMB : (n + 1) * DEMB] = mixed[n]

        pre = dot(inter[...], wheld[stage])
        value = whole[stage, me, span].astype(F32) + pre * jax.nn.sigmoid(pre)
        whole[stage + 1, me, span] = value.astype(BF16)
        begin(i + CHUNKS)

    def to_expert(d):
        to = (me + d) % n_dev
        return remote(outg.at[to], slot_grad.at[me], gsend.at[d], grecv.at[d], "tensor", to)

    for i in range(live, items):
        if i + RELAY < items:
            relay(i + RELAY)
            for e in range(4 + 2 * (i - live), 6 + 2 * (i - live)):
                cotangent(e)
        if i + FAR < items:
            relay_far(i + FAR)

    def send_cotangents():
        @pl.loop(1, n_dev)
        def _(d):
            to_expert(d).start()

    pl.when(core == 0)(send_cotangents)
    for i in range(live, items):
        complete(i)
    slot_grad[me] = outg[me]

    mine = (chosen(me, 0).astype(F32) + chosen(me, 1).astype(F32)).astype(BF16)
    for q in range(n_dev):
        rows_in[:, q * width : (q + 1) * width] = dot(mine, whole[2, q]).astype(BF16)
    eye = (
        lax.broadcasted_iota(jnp.int32, (width, width), 0)
        == lax.broadcasted_iota(jnp.int32, (width, width), 1)
    ).astype(F32).astype(BF16)
    for q in range(n_dev):
        rows_t[q * width : (q + 1) * width, :] = dot_nt(
            eye, rows_in[:, q * width : (q + 1) * width]
        ).astype(BF16)

    def partial(h, t, j):
        u, v = coord[h]
        owner = place(h, (u + (4 - sign[h]) * (1 + t)) % 4, (v + (4 - sign[h]) * (1 + j)) % 4)
        at = pl.ds(pl.multiple_of(owner * piece, piece), piece)
        return dot(rows_t[at, :], pgrad[:, h * part : (h + 1) * part])

    def hop1(h, k, src):
        u, v = coord[h]
        return remote(
            src, ring_buf.at[h, k], send1.at[h, k], recv1.at[h, k],
            "dp", place(h, (u + sign[h]) % 4, v),
        )

    def hop2(h, j):
        u, v = coord[h]
        return remote(
            ring_buf.at[h, 8 + j], last_buf.at[h, j],
            send2.at[h, j], recv2.at[h, j], "dp", place(h, u, (v + sign[h]) % 4),
        )

    def hop0(h, j, sub):
        u, v = coord[h]
        return remote(
            first_buf.at[h, sub, j], ring_buf.at[h, j, :, pl.ds(sub * width, width)],
            send0.at[h, sub, j], recv0.at[h, sub, j], "dp", place(h, (u + sign[h]) % 4, v),
        )

    for sub in range(2):
        for p in range(sub, n_dev, 2):
            if sub == 0:
                load_expert(p // 2).wait()
            pre = dot(rows_in[...], held[:, p * width : (p + 1) * width])
            sigma = jax.nn.sigmoid(pre)
            outs[p] = (pre * sigma).astype(BF16)
            slopes[p] = sigma + pre * sigma * (1.0 - sigma)
        if sub == 0:
            pl.when(core == 1)(send_cotangents)

        @pl.loop(1, n_dev)
        def _(d):
            source = (me + n_dev - d) % n_dev

            @pl.when(source % 2 == sub)
            def _():
                remote(
                    outg.at[me], slot_grad.at[source], gsend.at[d], grecv.at[d], "tensor", source
                ).wait_recv()

        for h in range(4):
            p = 2 * h + sub
            lanes = slice(p * width, (p + 1) * width)
            pgrad[:, lanes] = (slot_grad[p].astype(F32) * slopes[p]).astype(BF16)
            u, v = coord[h]

            @pl.loop(0, 4)
            def _(j):
                owner = place(h, (u + 4 - sign[h]) % 4, (v + (4 - sign[h]) * (1 + j)) % 4)
                at = pl.ds(pl.multiple_of(owner * piece, piece), piece)
                first_buf[h, sub, j] = dot(rows_t[at, :], pgrad[:, lanes]).astype(BF16)
                hop0(h, j, sub).start()

    def out_copy(d):
        to = (me + d) % n_dev
        return remote(outs.at[to], ret.at[me], osend.at[d], orecv.at[d], "tensor", to)

    @pl.loop(1, n_dev)
    def _(d):
        out_copy(d).start()

    ret[me] = outs[me]

    def ring_step(k, arrive):
        t, j = k // 4, k % 4
        own = [partial(h, t, j) for h in range(4)]
        for h in range(4):
            arrive(h, k - 4)
            ring_buf[h, k - 4] = (ring_buf[h, k - 4].astype(F32) + own[h]).astype(BF16)
            hop1(h, k, ring_buf.at[h, k - 4]).start()

    @pl.loop(4, 8)
    def _(k):
        def arrive(h, j):
            for sub in range(2):
                hop0(h, j, sub).wait_recv()

        ring_step(k, arrive)

    @pl.loop(1, n_dev)
    def _(d):
        source = (me + n_dev - d) % n_dev
        remote(
            outs.at[me], ret.at[source], osend.at[d], orecv.at[d], "tensor", source
        ).wait_recv()

    block_rows = 128

    @pl.loop(0, rows // block_rows)
    def _(b):
        at = pl.ds(pl.multiple_of(b * block_rows, block_rows), block_rows)
        seat = lax.broadcasted_iota(jnp.int32, (block_rows, cap), 1)
        picked = []
        for k in range(2):
            slot = cols[at, k : k + 1].astype(jnp.int32)
            total = jnp.zeros((block_rows, width), F32)
            for e in range(n_dev):
                hot = (slot == seat + e * cap).astype(F32).astype(BF16)
                total = total + dot(hot, ret[e])
            picked.append(total)
        for t in range(2):
            both = gate(at, t, 0) * picked[0] + gate(at, t, 1) * picked[1]
            mix[t, at, :] = both.astype(BF16)

    store_mix = pltpu.make_async_copy(mix, mix_out, lsem.at[0])
    store_mix.start()

    def store_wgrad(h):
        span = pl.ds(h * part, part)
        return pltpu.make_async_copy(wgrad.at[:, span], wgrad_out.at[:, span], wsem.at[h])

    @pl.loop(8, 12)
    def _(k):
        ring_step(k, lambda h, j: hop1(h, j, ring_buf.at[h, j]).wait_recv())

    for j in range(4):
        for h in range(4):
            own = partial(h, 3, j)
            hop1(h, 8 + j, ring_buf.at[h, 8 + j]).wait_recv()
            total = ring_buf[h, 8 + j].astype(F32) + own
            if j > 0:
                hop2(h, j - 1).wait_recv()
                total = total + last_buf[h, j - 1].astype(F32)
            if j < 3:
                ring_buf[h, 8 + j] = total.astype(BF16)
                hop2(h, j).start()
            else:
                wgrad[:, h * part : (h + 1) * part] = total
                store_wgrad(h).start()

    store_mix.wait()
    for h in range(4):
        store_wgrad(h).wait()

    @pl.loop(0, items)
    def _(i):
        for which in range(7):
            copy(i, which).wait_send()

    for h in range(4):
        @pl.loop(0, 4)
        def _(j):
            for sub in range(2):
                hop0(h, j, sub).wait_send()

        @pl.loop(4, 12)
        def _(k):
            hop1(h, k, ring_buf.at[h, k - 4]).wait_send()

        for j in range(3):
            hop2(h, j).wait_send()

    @pl.loop(1, n_dev)
    def _(d):
        to_expert(d).wait_send()
        out_copy(d).wait_send()


HBM = pl.BlockSpec(memory_space=pltpu.HBM)
DMA = pltpu.SemaphoreType.DMA


def on_device(
    embeddings, trunk_weights, trunk_gains, expert_weights, route_ids, task_gates, mixture_grad
):
    experts = lax.axis_size("tensor")
    rows, top = route_ids.shape
    cap = 2 * rows * top // experts
    width = embeddings.shape[1]
    full = width * experts
    step_rows = rows // CHUNKS
    piece = full // lax.axis_size("dp")
    by_slot = (experts, cap, width)

    mixture, weight_grad = pl.pallas_call(
        kernel,
        out_shape=(
            jax.ShapeDtypeStruct((2, rows, width), BF16),
            jax.ShapeDtypeStruct((piece, full), F32),
        ),
        in_specs=[HBM] * 7,
        out_specs=(HBM, HBM),
        scratch_shapes=[
            pltpu.VMEM((3, experts, rows, width), BF16),
            pltpu.VMEM((NEMB, step_rows, DEMB), BF16),
            pltpu.VMEM((step_rows, full), BF16),
            pltpu.VMEM((NEMB * GROUP, NEMB * GROUP), F32),
            pltpu.VMEM((2, full, width), BF16),
            pltpu.VMEM((2, rows, width), BF16),
            pltpu.VMEM((2, full), F32),
            pltpu.VMEM((top, rows), jnp.int32),
            pltpu.VMEM((2, top, rows), F32),
            pltpu.VMEM((2, rows, width), BF16),
            pltpu.VMEM(by_slot, BF16),
            pltpu.VMEM(by_slot, BF16),
            pltpu.VMEM((128, rows), F32),
            pltpu.VMEM((rows, 128), F32),
            pltpu.VMEM((full, full), BF16),
            pltpu.VMEM((cap, full), BF16),
            pltpu.VMEM((full, cap), BF16),
            pltpu.VMEM(by_slot, F32),
            pltpu.VMEM((cap, full), BF16),
            pltpu.VMEM(by_slot, BF16),
            pltpu.VMEM(by_slot, BF16),
            pltpu.VMEM((4, 2, 4, piece, width), BF16),
            pltpu.VMEM((4, 12, piece, full // 4), BF16),
            pltpu.VMEM((4, 3, piece, full // 4), BF16),
            pltpu.VMEM((2, rows, width), BF16),
            pltpu.VMEM((piece, full), F32),
            DMA((6,)),
            DMA((4,)),
            DMA((3 * CHUNKS, 7)),
            DMA((3 * CHUNKS, 7)),
            DMA((experts,)),
            DMA((experts,)),
            DMA((4, 12)),
            DMA((4, 12)),
            DMA((4, 3)),
            DMA((4, 3)),
            DMA((experts,)),
            DMA((experts,)),
            DMA((4, 2, 4)),
            DMA((4, 2, 4)),
        ],
        compiler_params=pltpu.CompilerParams(
            collective_id=0, has_side_effects=True, vmem_limit_bytes=56 << 20
        ),
        cost_estimate=pl.CostEstimate(flops=12 << 30, bytes_accessed=16 << 20, transcendentals=0),
        name="trunk_experts",
    )(
        embeddings, trunk_gains, trunk_weights, expert_weights[0], route_ids.T,
        task_gates.transpose(1, 2, 0), mixture_grad,
    )
    return (mixture, weight_grad[None])


def solution(mesh):
    in_specs = (
        P("dp", "tensor"),
        P(None, None, "tensor"),
        P(),
        P("tensor", None, None),
        P("dp", None),
        P("dp", None, None),
        P(None, "dp", "tensor"),
    )
    out_specs = (P(None, "dp", "tensor"), P("tensor", "dp", None))
    return jax.shard_map(
        on_device, mesh=mesh, in_specs=in_specs, out_specs=out_specs, check_vma=False
    )
```

```python
import math

import jax
import jax.numpy as jnp
from jax import lax
from jax.experimental import pallas as pl
from jax.experimental.pallas import tpu as pltpu
from jax.sharding import PartitionSpec as P

NEMB = 16
DEMB = 128
GROUP = 16
CHUNKS = 4
RELAY = 2
FAR = 1
F32 = jnp.float32
BF16 = jnp.bfloat16
MESH = pl.DeviceIdType.MESH


def dot(a, b):
    return jnp.dot(a, b, preferred_element_type=F32)


def dot_nt(a, b):
    return lax.dot_general(a, b, (((1,), (1,)), ((), ())), preferred_element_type=F32)


def remote(src, dst, send_sem, recv_sem, axis, index):
    return pltpu.make_async_remote_copy(
        src_ref=src, dst_ref=dst, send_sem=send_sem, recv_sem=recv_sem,
        device_id={axis: index}, device_id_type=MESH,
    )


def kernel(
    emb, gains_in, weights, experts_in, ids_in, gates_in, grad_in, mix_out, wgrad_out,
    whole, nrm, inter, mask, wheld, grad, gains, ids, gates, cot, outg, slot_grad, table, cols,
    held, rows_in, rows_t, slopes, pgrad, outs, ret, first_buf, ring_buf, last_buf,
    mix, wgrad, lsem, wsem, send, recv, gsend, grecv, send1, recv1, send2, recv2, osend, orecv, send0, recv0,
):
    n_dev, cap, width = outs.shape
    rows = emb.shape[0]
    piece, part = last_buf.shape[2:]
    items, live = 3 * CHUNKS, 2 * CHUNKS
    step_rows = rows // CHUNKS
    ring = n_dev // 2
    me = lax.axis_index("tensor")
    dp = lax.axis_index("dp")
    cx, cz = dp // 4, dp % 4
    y, core = me // 2, me % 2
    right = ((y + 1) % ring) * 2 + core
    left = ((y + ring - 1) % ring) * 2 + core
    far = ((y + 2) % ring) * 2 + core
    flip = 1 - 2 * core
    sib = me + flip

    load_emb = pltpu.make_async_copy(emb, whole.at[0, me], lsem.at[0])
    load_grad = pltpu.make_async_copy(grad_in, grad, lsem.at[1])
    load_weights = pltpu.make_async_copy(weights, wheld, lsem.at[2])
    load_gains = pltpu.make_async_copy(gains_in, gains, lsem.at[3])
    load_ids = pltpu.make_async_copy(ids_in, ids, lsem.at[4])
    load_gates = pltpu.make_async_copy(gates_in, gates, lsem.at[5])

    def load_expert(h):
        span = pl.ds(h * 2 * width, 2 * width)
        return pltpu.make_async_copy(experts_in.at[:, span], held.at[:, span], wsem.at[h])

    load_emb.start()
    for load in (load_ids, load_gates, load_gains, load_grad, load_weights):
        load.start()

    def place(h, u, v):
        return u * 4 + v if h < 2 else v * 4 + u

    barrier = pltpu.get_barrier_semaphore()
    peers = [("tensor", (me + d) % n_dev) for d in range(1, n_dev)] + [
        ("dp", place(0, (cx + 1) % 4, cz)), ("dp", place(0, (cx + 3) % 4, cz)),
        ("dp", place(0, cx, (cz + 1) % 4)), ("dp", place(0, cx, (cz + 3) % 4)),
    ]
    for axis, peer in peers:
        pl.semaphore_signal(barrier, inc=1, device_id={axis: peer}, device_id_type=MESH)

    def copy(i, which):
        turn = (i % 2) * (right - left)
        owner, to = (
            (me, sib), (me, right), (me, left), (left, sib), (right, sib),
            (left + turn, right - turn), (far, sib),
        )[which]
        at = pl.ds((i % CHUNKS) * step_rows, step_rows)
        ref = whole.at[i // CHUNKS, owner, at]
        return remote(ref, ref, send.at[i, which], recv.at[i, which], "tensor", to)

    def arrived(i, which):
        owner = (sib, left, right, left + flip, right + flip, far, far + flip)[which]
        at = pl.ds((i % CHUNKS) * step_rows, step_rows)
        ref = whole.at[i // CHUNKS, owner, at]
        remote(ref, ref, send.at[i, which], recv.at[i, which], "tensor", sib).wait_recv()

    def begin(i):
        for which in (1, 2, 0):
            copy(i, which).start()

        @pl.when(i >= live)
        def _():
            at = pl.ds((i % CHUNKS) * step_rows, step_rows)
            ref = whole.at[i // CHUNKS, me, at]
            remote(ref, ref, send.at[i, 5], recv.at[i, 5], "tensor", far).start()

    def relay(i):
        arrived(i, 1)
        arrived(i, 2)
        pl.when(i < live)(lambda: copy(i, 5).start())
        copy(i, 3).start()
        copy(i, 4).start()

    def relay_far(i):
        arrived(i, 5)
        copy(i, 6).start()

    def complete(i):
        for which in (0, 3, 4, 6):
            arrived(i, which)

    coord = [(cx, cz), (cx, cz), (cz, cx), (cz, cx)]
    sign = [1, 3, 1, 3]

    load_emb.wait()
    pl.semaphore_wait(barrier, len(peers))

    @pl.loop(0, CHUNKS)
    def _(i):
        begin(i)

    for h in range(4):
        load_expert(h).start()

    row_id = lax.broadcasted_iota(jnp.int32, mask.shape, 0) % GROUP
    col_id = lax.broadcasted_iota(jnp.int32, mask.shape, 1) % GROUP
    mask[...] = jnp.where(row_id == col_id, 1.0 / math.sqrt(DEMB * NEMB), 0.0)

    load_ids.wait()
    load_gates.wait()
    lane = lax.broadcasted_iota(jnp.int32, (n_dev, rows), 0)
    is_first = (ids[0:1, :] == lane).astype(F32)
    is_second = (ids[1:2, :] == lane).astype(F32)
    member = (is_first + is_second).astype(BF16)
    earlier = (
        lax.broadcasted_iota(jnp.int32, (rows, rows), 0)
        < lax.broadcasted_iota(jnp.int32, (rows, rows), 1)
    ).astype(F32).astype(BF16)
    slot_of = dot(member, earlier) + lane.astype(F32) * cap
    table[...] = jnp.zeros(table.shape, F32)
    table[0:1, :] = jnp.sum(is_first * slot_of, axis=0, keepdims=True)
    table[1:2, :] = jnp.sum(is_second * slot_of, axis=0, keepdims=True)
    for t in range(2):
        table[2 + 2 * t : 4 + 2 * t, :] = gates[t]
    cols[...] = table[...].T

    def gate(at, t, k):
        return cols[at, 2 + 2 * t + k : 3 + 2 * t + k]

    def chosen(expert, k):
        wanted = lax.broadcasted_iota(jnp.int32, (cap, rows), 0) + expert * cap
        return (table[k : k + 1, :].astype(jnp.int32) == wanted).astype(F32).astype(BF16)

    load_grad.wait()
    every = slice(0, rows)
    for k in range(2):
        cot[k] = (
            gate(every, 0, k) * grad[0].astype(F32) + gate(every, 1, k) * grad[1].astype(F32)
        ).astype(BF16)

    def cotangent(e):
        outg[e] = (dot(chosen(e, 0), cot[0]) + dot(chosen(e, 1), cot[1])).astype(BF16)

    for e in range(4):
        cotangent(e)
    for i in range(RELAY):
        relay(i)
        if 0 < i <= FAR:
            relay_far(i - 1)
    load_gains.wait()
    load_weights.wait()

    @pl.loop(0, live)
    def _(i):
        stage, first = i // CHUNKS, (i % CHUNKS) * step_rows
        span = pl.ds(pl.multiple_of(first, step_rows), step_rows)
        complete(i)

        def tile(n):
            return whole[stage, n // 2, span, (n % 2) * DEMB : (n % 2 + 1) * DEMB].astype(F32)

        total = jnp.zeros((step_rows, DEMB), F32)
        for n in range(NEMB):
            x = tile(n)
            total = total + x * x
        mean = jnp.sum(total, axis=1, keepdims=True) / (NEMB * DEMB)
        scale = lax.rsqrt(mean + 1e-05)
        for n in range(NEMB):
            lanes = slice(n * DEMB, (n + 1) * DEMB)
            gain = jnp.where(stage == 0, gains[0:1, lanes], gains[1:2, lanes])
            nrm[n] = (tile(n) * scale * gain).astype(BF16)
        relay(i + RELAY)
        passes = step_rows // GROUP // 4

        @pl.loop(0, passes)
        def _(g4):
            @pl.when(g4 == passes // 2)
            def _():
                relay_far(i + FAR)

            for g in range(4):
                at = pl.ds(pl.multiple_of((g4 * 4 + g) * GROUP, GROUP), GROUP)
                stack = nrm[:, at, :].reshape(NEMB * GROUP, DEMB)
                gram = (dot_nt(stack, stack) * mask[...]).astype(BF16)
                mixed = dot(gram, stack).astype(BF16)
                mixed = mixed.reshape(NEMB, GROUP, DEMB)
                for n in range(NEMB):
                    inter[at, n * DEMB : (n + 1) * DEMB] = mixed[n]

        pre = dot(inter[...], wheld[stage])
        value = whole[stage, me, span].astype(F32) + pre * jax.nn.sigmoid(pre)
        whole[stage + 1, me, span] = value.astype(BF16)
        begin(i + CHUNKS)

    def to_expert(d):
        to = (me + d) % n_dev
        return remote(outg.at[to], slot_grad.at[me], gsend.at[d], grecv.at[d], "tensor", to)

    for i in range(live, items):
        if i + RELAY < items:
            relay(i + RELAY)
            for e in range(4 + 2 * (i - live), 6 + 2 * (i - live)):
                cotangent(e)
        if i + FAR < items:
            relay_far(i + FAR)

    def send_cotangents():
        @pl.loop(1, n_dev)
        def _(d):
            to_expert(d).start()

    pl.when(core == 0)(send_cotangents)
    for i in range(live, items):
        complete(i)
    slot_grad[me] = outg[me]

    mine = (chosen(me, 0).astype(F32) + chosen(me, 1).astype(F32)).astype(BF16)
    for q in range(n_dev):
        rows_in[:, q * width : (q + 1) * width] = dot(mine, whole[2, q]).astype(BF16)
    eye = (
        lax.broadcasted_iota(jnp.int32, (width, width), 0)
        == lax.broadcasted_iota(jnp.int32, (width, width), 1)
    ).astype(F32).astype(BF16)
    for q in range(n_dev):
        rows_t[q * width : (q + 1) * width, :] = dot_nt(
            eye, rows_in[:, q * width : (q + 1) * width]
        ).astype(BF16)

    def partial(h, t, j):
        u, v = coord[h]
        owner = place(h, (u + (4 - sign[h]) * (1 + t)) % 4, (v + (4 - sign[h]) * (1 + j)) % 4)
        at = pl.ds(pl.multiple_of(owner * piece, piece), piece)
        return dot(rows_t[at, :], pgrad[:, h * part : (h + 1) * part])

    def hop1(h, k, src):
        u, v = coord[h]
        return remote(
            src, ring_buf.at[h, k], send1.at[h, k], recv1.at[h, k],
            "dp", place(h, (u + sign[h]) % 4, v),
        )

    def hop2(h, j):
        u, v = coord[h]
        return remote(
            ring_buf.at[h, 8 + j], last_buf.at[h, j],
            send2.at[h, j], recv2.at[h, j], "dp", place(h, u, (v + sign[h]) % 4),
        )

    def hop0(h, j, sub):
        u, v = coord[h]
        return remote(
            first_buf.at[h, sub, j], ring_buf.at[h, j, :, pl.ds(sub * width, width)],
            send0.at[h, sub, j], recv0.at[h, sub, j], "dp", place(h, (u + sign[h]) % 4, v),
        )

    for sub in range(2):
        for p in range(sub, n_dev, 2):
            if sub == 0:
                load_expert(p // 2).wait()
            pre = dot(rows_in[...], held[:, p * width : (p + 1) * width])
            sigma = jax.nn.sigmoid(pre)
            outs[p] = (pre * sigma).astype(BF16)
            slopes[p] = sigma + pre * sigma * (1.0 - sigma)
        if sub == 0:
            pl.when(core == 1)(send_cotangents)

        @pl.loop(1, n_dev)
        def _(d):
            source = (me + n_dev - d) % n_dev

            @pl.when(source % 2 == sub)
            def _():
                remote(
                    outg.at[me], slot_grad.at[source], gsend.at[d], grecv.at[d], "tensor", source
                ).wait_recv()

        for h in range(4):
            p = 2 * h + sub
            lanes = slice(p * width, (p + 1) * width)
            pgrad[:, lanes] = (slot_grad[p].astype(F32) * slopes[p]).astype(BF16)
            u, v = coord[h]

            @pl.loop(0, 4)
            def _(j):
                owner = place(h, (u + 4 - sign[h]) % 4, (v + (4 - sign[h]) * (1 + j)) % 4)
                at = pl.ds(pl.multiple_of(owner * piece, piece), piece)
                first_buf[h, sub, j] = dot(rows_t[at, :], pgrad[:, lanes]).astype(BF16)
                hop0(h, j, sub).start()

    def out_copy(d):
        to = (me + d) % n_dev
        return remote(outs.at[to], ret.at[me], osend.at[d], orecv.at[d], "tensor", to)

    @pl.loop(1, n_dev)
    def _(d):
        out_copy(d).start()

    ret[me] = outs[me]

    def ring_step(k, arrive):
        t, j = k // 4, k % 4
        own = [partial(h, t, j) for h in range(4)]
        for h in range(4):
            arrive(h, k - 4)
            ring_buf[h, k - 4] = (ring_buf[h, k - 4].astype(F32) + own[h]).astype(BF16)
            hop1(h, k, ring_buf.at[h, k - 4]).start()

    @pl.loop(4, 8)
    def _(k):
        def arrive(h, j):
            for sub in range(2):
                hop0(h, j, sub).wait_recv()

        ring_step(k, arrive)

    @pl.loop(1, n_dev)
    def _(d):
        source = (me + n_dev - d) % n_dev
        remote(
            outs.at[me], ret.at[source], osend.at[d], orecv.at[d], "tensor", source
        ).wait_recv()

    block_rows = 128

    @pl.loop(0, rows // block_rows)
    def _(b):
        at = pl.ds(pl.multiple_of(b * block_rows, block_rows), block_rows)
        seat = lax.broadcasted_iota(jnp.int32, (block_rows, cap), 1)
        picked = []
        for k in range(2):
            slot = cols[at, k : k + 1].astype(jnp.int32)
            total = jnp.zeros((block_rows, width), F32)
            for e in range(n_dev):
                hot = (slot == seat + e * cap).astype(F32).astype(BF16)
                total = total + dot(hot, ret[e])
            picked.append(total)
        for t in range(2):
            both = gate(at, t, 0) * picked[0] + gate(at, t, 1) * picked[1]
            mix[t, at, :] = both.astype(BF16)

    store_mix = pltpu.make_async_copy(mix, mix_out, lsem.at[0])
    store_mix.start()

    def store_wgrad(h):
        span = pl.ds(h * part, part)
        return pltpu.make_async_copy(wgrad.at[:, span], wgrad_out.at[:, span], wsem.at[h])

    @pl.loop(8, 12)
    def _(k):
        ring_step(k, lambda h, j: hop1(h, j, ring_buf.at[h, j]).wait_recv())

    for j in range(4):
        own = [partial(h, 3, j) for h in range(4)]
        for h in range(4):
            hop1(h, 8 + j, ring_buf.at[h, 8 + j]).wait_recv()
            total = ring_buf[h, 8 + j].astype(F32) + own[h]
            if j > 0:
                hop2(h, j - 1).wait_recv()
                total = total + last_buf[h, j - 1].astype(F32)
            if j < 3:
                ring_buf[h, 8 + j] = total.astype(BF16)
                hop2(h, j).start()
            else:
                wgrad[:, h * part : (h + 1) * part] = total
                store_wgrad(h).start()

    store_mix.wait()
    for h in range(4):
        store_wgrad(h).wait()

    @pl.loop(0, items)
    def _(i):
        for which in range(7):
            copy(i, which).wait_send()

    for h in range(4):
        @pl.loop(0, 4)
        def _(j):
            for sub in range(2):
                hop0(h, j, sub).wait_send()

        @pl.loop(4, 12)
        def _(k):
            hop1(h, k, ring_buf.at[h, k - 4]).wait_send()

        for j in range(3):
            hop2(h, j).wait_send()

    @pl.loop(1, n_dev)
    def _(d):
        to_expert(d).wait_send()
        out_copy(d).wait_send()


HBM = pl.BlockSpec(memory_space=pltpu.HBM)
DMA = pltpu.SemaphoreType.DMA


def on_device(
    embeddings, trunk_weights, trunk_gains, expert_weights, route_ids, task_gates, mixture_grad
):
    experts = lax.axis_size("tensor")
    rows, top = route_ids.shape
    cap = 2 * rows * top // experts
    width = embeddings.shape[1]
    full = width * experts
    step_rows = rows // CHUNKS
    piece = full // lax.axis_size("dp")
    by_slot = (experts, cap, width)

    mixture, weight_grad = pl.pallas_call(
        kernel,
        out_shape=(
            jax.ShapeDtypeStruct((2, rows, width), BF16),
            jax.ShapeDtypeStruct((piece, full), F32),
        ),
        in_specs=[HBM] * 7,
        out_specs=(HBM, HBM),
        scratch_shapes=[
            pltpu.VMEM((3, experts, rows, width), BF16),
            pltpu.VMEM((NEMB, step_rows, DEMB), BF16),
            pltpu.VMEM((step_rows, full), BF16),
            pltpu.VMEM((NEMB * GROUP, NEMB * GROUP), F32),
            pltpu.VMEM((2, full, width), BF16),
            pltpu.VMEM((2, rows, width), BF16),
            pltpu.VMEM((2, full), F32),
            pltpu.VMEM((top, rows), jnp.int32),
            pltpu.VMEM((2, top, rows), F32),
            pltpu.VMEM((2, rows, width), BF16),
            pltpu.VMEM(by_slot, BF16),
            pltpu.VMEM(by_slot, BF16),
            pltpu.VMEM((128, rows), F32),
            pltpu.VMEM((rows, 128), F32),
            pltpu.VMEM((full, full), BF16),
            pltpu.VMEM((cap, full), BF16),
            pltpu.VMEM((full, cap), BF16),
            pltpu.VMEM(by_slot, F32),
            pltpu.VMEM((cap, full), BF16),
            pltpu.VMEM(by_slot, BF16),
            pltpu.VMEM(by_slot, BF16),
            pltpu.VMEM((4, 2, 4, piece, width), BF16),
            pltpu.VMEM((4, 12, piece, full // 4), BF16),
            pltpu.VMEM((4, 3, piece, full // 4), BF16),
            pltpu.VMEM((2, rows, width), BF16),
            pltpu.VMEM((piece, full), F32),
            DMA((6,)),
            DMA((4,)),
            DMA((3 * CHUNKS, 7)),
            DMA((3 * CHUNKS, 7)),
            DMA((experts,)),
            DMA((experts,)),
            DMA((4, 12)),
            DMA((4, 12)),
            DMA((4, 3)),
            DMA((4, 3)),
            DMA((experts,)),
            DMA((experts,)),
            DMA((4, 2, 4)),
            DMA((4, 2, 4)),
        ],
        compiler_params=pltpu.CompilerParams(
            collective_id=0, has_side_effects=True, vmem_limit_bytes=56 << 20
        ),
        cost_estimate=pl.CostEstimate(flops=12 << 30, bytes_accessed=16 << 20, transcendentals=0),
        name="trunk_experts",
    )(
        embeddings, trunk_gains, trunk_weights, expert_weights[0], route_ids.T,
        task_gates.transpose(1, 2, 0), mixture_grad,
    )
    return (mixture, weight_grad[None])


def solution(mesh):
    in_specs = (
        P("dp", "tensor"),
        P(None, None, "tensor"),
        P(),
        P("tensor", None, None),
        P("dp", None),
        P("dp", None, None),
        P(None, "dp", "tensor"),
    )
    out_specs = (P(None, "dp", "tensor"), P("tensor", "dp", None))
    return jax.shard_map(
        on_device, mesh=mesh, in_specs=in_specs, out_specs=out_specs, check_vma=False
    )
```

```python
import math

import jax
import jax.numpy as jnp
from jax import lax
from jax.experimental import pallas as pl
from jax.experimental.pallas import tpu as pltpu
from jax.sharding import PartitionSpec as P

NEMB = 16
DEMB = 128
GROUP = 16
CHUNKS = 4
RELAY = 2
FAR = 1
F32 = jnp.float32
BF16 = jnp.bfloat16
MESH = pl.DeviceIdType.MESH


def dot(a, b):
    return jnp.dot(a, b, preferred_element_type=F32)


def dot_nt(a, b):
    return lax.dot_general(a, b, (((1,), (1,)), ((), ())), preferred_element_type=F32)


def remote(src, dst, send_sem, recv_sem, axis, index):
    return pltpu.make_async_remote_copy(
        src_ref=src, dst_ref=dst, send_sem=send_sem, recv_sem=recv_sem,
        device_id={axis: index}, device_id_type=MESH,
    )


def kernel(
    emb, gains_in, weights, experts_in, ids_in, gates_in, grad_in, mix_out, wgrad_out,
    whole, nrm, inter, mask, wheld, grad, gains, ids, gates, cot, outg, slot_grad, table, cols,
    held, rows_in, rows_t, slopes, pgrad, outs, ret, first_buf, ring_buf, last_buf,
    mix, wgrad, lsem, wsem, send, recv, gsend, grecv, send1, recv1, send2, recv2, osend, orecv, send0, recv0,
):
    n_dev, cap, width = outs.shape
    rows = emb.shape[0]
    piece, part = last_buf.shape[2:]
    items, live = 3 * CHUNKS, 2 * CHUNKS
    step_rows = rows // CHUNKS
    ring = n_dev // 2
    me = lax.axis_index("tensor")
    dp = lax.axis_index("dp")
    cx, cz = dp // 4, dp % 4
    y, core = me // 2, me % 2
    right = ((y + 1) % ring) * 2 + core
    left = ((y + ring - 1) % ring) * 2 + core
    far = ((y + 2) % ring) * 2 + core
    flip = 1 - 2 * core
    sib = me + flip

    load_emb = pltpu.make_async_copy(emb, whole.at[0, me], lsem.at[0])
    load_grad = pltpu.make_async_copy(grad_in, grad, lsem.at[1])
    load_weights = pltpu.make_async_copy(weights, wheld, lsem.at[2])
    load_gains = pltpu.make_async_copy(gains_in, gains, lsem.at[3])
    load_ids = pltpu.make_async_copy(ids_in, ids, lsem.at[4])
    load_gates = pltpu.make_async_copy(gates_in, gates, lsem.at[5])

    def load_expert(h):
        span = pl.ds(h * 2 * width, 2 * width)
        return pltpu.make_async_copy(experts_in.at[:, span], held.at[:, span], wsem.at[h])

    load_emb.start()
    for load in (load_ids, load_gates, load_gains, load_grad, load_weights):
        load.start()

    def place(h, u, v):
        return u * 4 + v if h < 2 else v * 4 + u

    barrier = pltpu.get_barrier_semaphore()
    peers = [("tensor", (me + d) % n_dev) for d in range(1, n_dev)] + [
        ("dp", place(0, (cx + 1) % 4, cz)), ("dp", place(0, (cx + 3) % 4, cz)),
        ("dp", place(0, cx, (cz + 1) % 4)), ("dp", place(0, cx, (cz + 3) % 4)),
    ]
    for axis, peer in peers:
        pl.semaphore_signal(barrier, inc=1, device_id={axis: peer}, device_id_type=MESH)

    def copy(i, which):
        turn = (i % 2) * (right - left)
        owner, to = (
            (me, sib), (me, right), (me, left), (left, sib), (right, sib),
            (left + turn, right - turn), (far, sib),
        )[which]
        at = pl.ds((i % CHUNKS) * step_rows, step_rows)
        ref = whole.at[i // CHUNKS, owner, at]
        return remote(ref, ref, send.at[i, which], recv.at[i, which], "tensor", to)

    def arrived(i, which):
        owner = (sib, left, right, left + flip, right + flip, far, far + flip)[which]
        at = pl.ds((i % CHUNKS) * step_rows, step_rows)
        ref = whole.at[i // CHUNKS, owner, at]
        remote(ref, ref, send.at[i, which], recv.at[i, which], "tensor", sib).wait_recv()

    def begin(i):
        @pl.when(i >= live)
        def _():
            at = pl.ds((i % CHUNKS) * step_rows, step_rows)
            ref = whole.at[i // CHUNKS, me, at]
            remote(ref, ref, send.at[i, 5], recv.at[i, 5], "tensor", far).start()

        for which in (1, 2, 0):
            copy(i, which).start()

    def relay(i):
        arrived(i, 1)
        arrived(i, 2)
        pl.when(i < live)(lambda: copy(i, 5).start())
        copy(i, 3).start()
        copy(i, 4).start()

    def relay_far(i):
        arrived(i, 5)
        copy(i, 6).start()

    def complete(i):
        for which in (0, 3, 4, 6):
            arrived(i, which)

    coord = [(cx, cz), (cx, cz), (cz, cx), (cz, cx)]
    sign = [1, 3, 1, 3]

    load_emb.wait()
    pl.semaphore_wait(barrier, len(peers))

    @pl.loop(0, CHUNKS)
    def _(i):
        begin(i)

    for h in range(4):
        load_expert(h).start()

    row_id = lax.broadcasted_iota(jnp.int32, mask.shape, 0) % GROUP
    col_id = lax.broadcasted_iota(jnp.int32, mask.shape, 1) % GROUP
    mask[...] = jnp.where(row_id == col_id, 1.0 / math.sqrt(DEMB * NEMB), 0.0)

    load_ids.wait()
    load_gates.wait()
    lane = lax.broadcasted_iota(jnp.int32, (n_dev, rows), 0)
    is_first = (ids[0:1, :] == lane).astype(F32)
    is_second = (ids[1:2, :] == lane).astype(F32)
    member = (is_first + is_second).astype(BF16)
    earlier = (
        lax.broadcasted_iota(jnp.int32, (rows, rows), 0)
        < lax.broadcasted_iota(jnp.int32, (rows, rows), 1)
    ).astype(F32).astype(BF16)
    slot_of = dot(member, earlier) + lane.astype(F32) * cap
    table[...] = jnp.zeros(table.shape, F32)
    table[0:1, :] = jnp.sum(is_first * slot_of, axis=0, keepdims=True)
    table[1:2, :] = jnp.sum(is_second * slot_of, axis=0, keepdims=True)
    for t in range(2):
        table[2 + 2 * t : 4 + 2 * t, :] = gates[t]
    cols[...] = table[...].T

    def gate(at, t, k):
        return cols[at, 2 + 2 * t + k : 3 + 2 * t + k]

    def chosen(expert, k):
        wanted = lax.broadcasted_iota(jnp.int32, (cap, rows), 0) + expert * cap
        return (table[k : k + 1, :].astype(jnp.int32) == wanted).astype(F32).astype(BF16)

    load_grad.wait()
    every = slice(0, rows)
    for k in range(2):
        cot[k] = (
            gate(every, 0, k) * grad[0].astype(F32) + gate(every, 1, k) * grad[1].astype(F32)
        ).astype(BF16)

    def cotangent(e):
        outg[e] = (dot(chosen(e, 0), cot[0]) + dot(chosen(e, 1), cot[1])).astype(BF16)

    for e in range(4):
        cotangent(e)
    for i in range(RELAY):
        relay(i)
        if 0 < i <= FAR:
            relay_far(i - 1)
    load_gains.wait()
    load_weights.wait()

    @pl.loop(0, live)
    def _(i):
        stage, first = i // CHUNKS, (i % CHUNKS) * step_rows
        span = pl.ds(pl.multiple_of(first, step_rows), step_rows)
        complete(i)

        def tile(n):
            return whole[stage, n // 2, span, (n % 2) * DEMB : (n % 2 + 1) * DEMB].astype(F32)

        total = jnp.zeros((step_rows, DEMB), F32)
        for n in range(NEMB):
            x = tile(n)
            total = total + x * x
        mean = jnp.sum(total, axis=1, keepdims=True) / (NEMB * DEMB)
        scale = lax.rsqrt(mean + 1e-05)
        for n in range(NEMB):
            lanes = slice(n * DEMB, (n + 1) * DEMB)
            gain = jnp.where(stage == 0, gains[0:1, lanes], gains[1:2, lanes])
            nrm[n] = (tile(n) * scale * gain).astype(BF16)
        relay(i + RELAY)
        passes = step_rows // GROUP // 4

        @pl.loop(0, passes)
        def _(g4):
            @pl.when(g4 == passes // 2)
            def _():
                relay_far(i + FAR)

            for g in range(4):
                at = pl.ds(pl.multiple_of((g4 * 4 + g) * GROUP, GROUP), GROUP)
                stack = nrm[:, at, :].reshape(NEMB * GROUP, DEMB)
                gram = (dot_nt(stack, stack) * mask[...]).astype(BF16)
                mixed = dot(gram, stack).astype(BF16)
                mixed = mixed.reshape(NEMB, GROUP, DEMB)
                for n in range(NEMB):
                    inter[at, n * DEMB : (n + 1) * DEMB] = mixed[n]

        pre = dot(inter[...], wheld[stage])
        value = whole[stage, me, span].astype(F32) + pre * jax.nn.sigmoid(pre)
        whole[stage + 1, me, span] = value.astype(BF16)
        begin(i + CHUNKS)

    def to_expert(d):
        to = (me + d) % n_dev
        return remote(outg.at[to], slot_grad.at[me], gsend.at[d], grecv.at[d], "tensor", to)

    for i in range(live, items):
        if i + RELAY < items:
            relay(i + RELAY)
            for e in range(4 + 2 * (i - live), 6 + 2 * (i - live)):
                cotangent(e)
        if i + FAR < items:
            relay_far(i + FAR)

    def send_cotangents():
        @pl.loop(1, n_dev)
        def _(d):
            to_expert(d).start()

    pl.when(core == 0)(send_cotangents)
    for i in range(live, items):
        complete(i)
    slot_grad[me] = outg[me]

    mine = (chosen(me, 0).astype(F32) + chosen(me, 1).astype(F32)).astype(BF16)
    for q in range(n_dev):
        rows_in[:, q * width : (q + 1) * width] = dot(mine, whole[2, q]).astype(BF16)
    eye = (
        lax.broadcasted_iota(jnp.int32, (width, width), 0)
        == lax.broadcasted_iota(jnp.int32, (width, width), 1)
    ).astype(F32).astype(BF16)
    for q in range(n_dev):
        rows_t[q * width : (q + 1) * width, :] = dot_nt(
            eye, rows_in[:, q * width : (q + 1) * width]
        ).astype(BF16)

    def partial(h, t, j):
        u, v = coord[h]
        owner = place(h, (u + (4 - sign[h]) * (1 + t)) % 4, (v + (4 - sign[h]) * (1 + j)) % 4)
        at = pl.ds(pl.multiple_of(owner * piece, piece), piece)
        return dot(rows_t[at, :], pgrad[:, h * part : (h + 1) * part])

    def hop1(h, k, src):
        u, v = coord[h]
        return remote(
            src, ring_buf.at[h, k], send1.at[h, k], recv1.at[h, k],
            "dp", place(h, (u + sign[h]) % 4, v),
        )

    def hop2(h, j):
        u, v = coord[h]
        return remote(
            ring_buf.at[h, 8 + j], last_buf.at[h, j],
            send2.at[h, j], recv2.at[h, j], "dp", place(h, u, (v + sign[h]) % 4),
        )

    def hop0(h, j, sub):
        u, v = coord[h]
        return remote(
            first_buf.at[h, sub, j], ring_buf.at[h, j, :, pl.ds(sub * width, width)],
            send0.at[h, sub, j], recv0.at[h, sub, j], "dp", place(h, (u + sign[h]) % 4, v),
        )

    for sub in range(2):
        for p in range(sub, n_dev, 2):
            if sub == 0:
                load_expert(p // 2).wait()
            pre = dot(rows_in[...], held[:, p * width : (p + 1) * width])
            sigma = jax.nn.sigmoid(pre)
            outs[p] = (pre * sigma).astype(BF16)
            slopes[p] = sigma + pre * sigma * (1.0 - sigma)
        if sub == 0:
            pl.when(core == 1)(send_cotangents)

        @pl.loop(1, n_dev)
        def _(d):
            source = (me + n_dev - d) % n_dev

            @pl.when(source % 2 == sub)
            def _():
                remote(
                    outg.at[me], slot_grad.at[source], gsend.at[d], grecv.at[d], "tensor", source
                ).wait_recv()

        for h in range(4):
            p = 2 * h + sub
            lanes = slice(p * width, (p + 1) * width)
            pgrad[:, lanes] = (slot_grad[p].astype(F32) * slopes[p]).astype(BF16)
            u, v = coord[h]

            @pl.loop(0, 4)
            def _(j):
                owner = place(h, (u + 4 - sign[h]) % 4, (v + (4 - sign[h]) * (1 + j)) % 4)
                at = pl.ds(pl.multiple_of(owner * piece, piece), piece)
                first_buf[h, sub, j] = dot(rows_t[at, :], pgrad[:, lanes]).astype(BF16)
                hop0(h, j, sub).start()

    def out_copy(d):
        to = (me + d) % n_dev
        return remote(outs.at[to], ret.at[me], osend.at[d], orecv.at[d], "tensor", to)

    @pl.loop(1, n_dev)
    def _(d):
        out_copy(d).start()

    ret[me] = outs[me]

    def ring_step(k, arrive):
        t, j = k // 4, k % 4
        own = [partial(h, t, j) for h in range(4)]
        for h in range(4):
            arrive(h, k - 4)
            ring_buf[h, k - 4] = (ring_buf[h, k - 4].astype(F32) + own[h]).astype(BF16)
            hop1(h, k, ring_buf.at[h, k - 4]).start()

    @pl.loop(4, 8)
    def _(k):
        def arrive(h, j):
            for sub in range(2):
                hop0(h, j, sub).wait_recv()

        ring_step(k, arrive)

    @pl.loop(1, n_dev)
    def _(d):
        source = (me + n_dev - d) % n_dev
        remote(
            outs.at[me], ret.at[source], osend.at[d], orecv.at[d], "tensor", source
        ).wait_recv()

    block_rows = 128

    @pl.loop(0, rows // block_rows)
    def _(b):
        at = pl.ds(pl.multiple_of(b * block_rows, block_rows), block_rows)
        seat = lax.broadcasted_iota(jnp.int32, (block_rows, cap), 1)
        picked = []
        for k in range(2):
            slot = cols[at, k : k + 1].astype(jnp.int32)
            total = jnp.zeros((block_rows, width), F32)
            for e in range(n_dev):
                hot = (slot == seat + e * cap).astype(F32).astype(BF16)
                total = total + dot(hot, ret[e])
            picked.append(total)
        for t in range(2):
            both = gate(at, t, 0) * picked[0] + gate(at, t, 1) * picked[1]
            mix[t, at, :] = both.astype(BF16)

    store_mix = pltpu.make_async_copy(mix, mix_out, lsem.at[0])
    store_mix.start()

    def store_wgrad(h):
        span = pl.ds(h * part, part)
        return pltpu.make_async_copy(wgrad.at[:, span], wgrad_out.at[:, span], wsem.at[h])

    @pl.loop(8, 12)
    def _(k):
        ring_step(k, lambda h, j: hop1(h, j, ring_buf.at[h, j]).wait_recv())

    for j in range(4):
        own = [partial(h, 3, j) for h in range(4)]
        for h in range(4):
            hop1(h, 8 + j, ring_buf.at[h, 8 + j]).wait_recv()
            total = ring_buf[h, 8 + j].astype(F32) + own[h]
            if j > 0:
                hop2(h, j - 1).wait_recv()
                total = total + last_buf[h, j - 1].astype(F32)
            if j < 3:
                ring_buf[h, 8 + j] = total.astype(BF16)
                hop2(h, j).start()
            else:
                wgrad[:, h * part : (h + 1) * part] = total
                store_wgrad(h).start()

    store_mix.wait()
    for h in range(4):
        store_wgrad(h).wait()

    @pl.loop(0, items)
    def _(i):
        for which in range(7):
            copy(i, which).wait_send()

    for h in range(4):
        @pl.loop(0, 4)
        def _(j):
            for sub in range(2):
                hop0(h, j, sub).wait_send()

        @pl.loop(4, 12)
        def _(k):
            hop1(h, k, ring_buf.at[h, k - 4]).wait_send()

        for j in range(3):
            hop2(h, j).wait_send()

    @pl.loop(1, n_dev)
    def _(d):
        to_expert(d).wait_send()
        out_copy(d).wait_send()


HBM = pl.BlockSpec(memory_space=pltpu.HBM)
DMA = pltpu.SemaphoreType.DMA


def on_device(
    embeddings, trunk_weights, trunk_gains, expert_weights, route_ids, task_gates, mixture_grad
):
    experts = lax.axis_size("tensor")
    rows, top = route_ids.shape
    cap = 2 * rows * top // experts
    width = embeddings.shape[1]
    full = width * experts
    step_rows = rows // CHUNKS
    piece = full // lax.axis_size("dp")
    by_slot = (experts, cap, width)

    mixture, weight_grad = pl.pallas_call(
        kernel,
        out_shape=(
            jax.ShapeDtypeStruct((2, rows, width), BF16),
            jax.ShapeDtypeStruct((piece, full), F32),
        ),
        in_specs=[HBM] * 7,
        out_specs=(HBM, HBM),
        scratch_shapes=[
            pltpu.VMEM((3, experts, rows, width), BF16),
            pltpu.VMEM((NEMB, step_rows, DEMB), BF16),
            pltpu.VMEM((step_rows, full), BF16),
            pltpu.VMEM((NEMB * GROUP, NEMB * GROUP), F32),
            pltpu.VMEM((2, full, width), BF16),
            pltpu.VMEM((2, rows, width), BF16),
            pltpu.VMEM((2, full), F32),
            pltpu.VMEM((top, rows), jnp.int32),
            pltpu.VMEM((2, top, rows), F32),
            pltpu.VMEM((2, rows, width), BF16),
            pltpu.VMEM(by_slot, BF16),
            pltpu.VMEM(by_slot, BF16),
            pltpu.VMEM((128, rows), F32),
            pltpu.VMEM((rows, 128), F32),
            pltpu.VMEM((full, full), BF16),
            pltpu.VMEM((cap, full), BF16),
            pltpu.VMEM((full, cap), BF16),
            pltpu.VMEM(by_slot, F32),
            pltpu.VMEM((cap, full), BF16),
            pltpu.VMEM(by_slot, BF16),
            pltpu.VMEM(by_slot, BF16),
            pltpu.VMEM((4, 2, 4, piece, width), BF16),
            pltpu.VMEM((4, 12, piece, full // 4), BF16),
            pltpu.VMEM((4, 3, piece, full // 4), BF16),
            pltpu.VMEM((2, rows, width), BF16),
            pltpu.VMEM((piece, full), F32),
            DMA((6,)),
            DMA((4,)),
            DMA((3 * CHUNKS, 7)),
            DMA((3 * CHUNKS, 7)),
            DMA((experts,)),
            DMA((experts,)),
            DMA((4, 12)),
            DMA((4, 12)),
            DMA((4, 3)),
            DMA((4, 3)),
            DMA((experts,)),
            DMA((experts,)),
            DMA((4, 2, 4)),
            DMA((4, 2, 4)),
        ],
        compiler_params=pltpu.CompilerParams(
            collective_id=0, has_side_effects=True, vmem_limit_bytes=56 << 20
        ),
        cost_estimate=pl.CostEstimate(flops=12 << 30, bytes_accessed=16 << 20, transcendentals=0),
        name="trunk_experts",
    )(
        embeddings, trunk_gains, trunk_weights, expert_weights[0], route_ids.T,
        task_gates.transpose(1, 2, 0), mixture_grad,
    )
    return (mixture, weight_grad[None])


def solution(mesh):
    in_specs = (
        P("dp", "tensor"),
        P(None, None, "tensor"),
        P(),
        P("tensor", None, None),
        P("dp", None),
        P("dp", None, None),
        P(None, "dp", "tensor"),
    )
    out_specs = (P(None, "dp", "tensor"), P("tensor", "dp", None))
    return jax.shard_map(
        on_device, mesh=mesh, in_specs=in_specs, out_specs=out_specs, check_vma=False
    )
```

```python
import math

import jax
import jax.numpy as jnp
from jax import lax
from jax.experimental import pallas as pl
from jax.experimental.pallas import tpu as pltpu
from jax.sharding import PartitionSpec as P

NEMB = 16
DEMB = 128
GROUP = 16
CHUNKS = 4
RELAY = 2
FAR = 1
F32 = jnp.float32
BF16 = jnp.bfloat16
MESH = pl.DeviceIdType.MESH


def dot(a, b):
    return jnp.dot(a, b, preferred_element_type=F32)


def dot_nt(a, b):
    return lax.dot_general(a, b, (((1,), (1,)), ((), ())), preferred_element_type=F32)


def remote(src, dst, send_sem, recv_sem, axis, index):
    return pltpu.make_async_remote_copy(
        src_ref=src, dst_ref=dst, send_sem=send_sem, recv_sem=recv_sem,
        device_id={axis: index}, device_id_type=MESH,
    )


def kernel(
    emb, gains_in, weights, experts_in, ids_in, gates_in, grad_in, mix_out, wgrad_out,
    whole, nrm, inter, mask, wheld, grad, gains, ids, gates, cot, outg, slot_grad, table, cols,
    held, rows_in, rows_t, slopes, pgrad, outs, ret, first_buf, ring_buf, last_buf,
    mix, wgrad, lsem, wsem, send, recv, gsend, grecv, send1, recv1, send2, recv2, osend, orecv, send0, recv0,
):
    n_dev, cap, width = outs.shape
    rows = emb.shape[0]
    piece, part = last_buf.shape[2:]
    items, live = 3 * CHUNKS, 2 * CHUNKS
    step_rows = rows // CHUNKS
    ring = n_dev // 2
    me = lax.axis_index("tensor")
    dp = lax.axis_index("dp")
    cx, cz = dp // 4, dp % 4
    y, core = me // 2, me % 2
    right = ((y + 1) % ring) * 2 + core
    left = ((y + ring - 1) % ring) * 2 + core
    far = ((y + 2) % ring) * 2 + core
    flip = 1 - 2 * core
    sib = me + flip

    load_emb = pltpu.make_async_copy(emb, whole.at[0, me], lsem.at[0])
    load_grad = pltpu.make_async_copy(grad_in, grad, lsem.at[1])
    load_weights = pltpu.make_async_copy(weights, wheld, lsem.at[2])
    load_gains = pltpu.make_async_copy(gains_in, gains, lsem.at[3])
    load_ids = pltpu.make_async_copy(ids_in, ids, lsem.at[4])
    load_gates = pltpu.make_async_copy(gates_in, gates, lsem.at[5])

    def load_expert(h):
        span = pl.ds(h * 2 * width, 2 * width)
        return pltpu.make_async_copy(experts_in.at[:, span], held.at[:, span], wsem.at[h])

    load_emb.start()
    for load in (load_ids, load_gates, load_gains, load_grad, load_weights):
        load.start()

    def place(h, u, v):
        return u * 4 + v if h < 2 else v * 4 + u

    barrier = pltpu.get_barrier_semaphore()
    peers = [("tensor", (me + d) % n_dev) for d in range(1, n_dev)] + [
        ("dp", place(0, (cx + 1) % 4, cz)), ("dp", place(0, (cx + 3) % 4, cz)),
        ("dp", place(0, cx, (cz + 1) % 4)), ("dp", place(0, cx, (cz + 3) % 4)),
    ]
    for axis, peer in peers:
        pl.semaphore_signal(barrier, inc=1, device_id={axis: peer}, device_id_type=MESH)

    def copy(i, which):
        turn = (i % 2) * (right - left)
        owner, to = (
            (me, sib), (me, right), (me, left), (left, sib), (right, sib),
            (left + turn, right - turn), (far, sib),
        )[which]
        at = pl.ds((i % CHUNKS) * step_rows, step_rows)
        ref = whole.at[i // CHUNKS, owner, at]
        return remote(ref, ref, send.at[i, which], recv.at[i, which], "tensor", to)

    def arrived(i, which):
        owner = (sib, left, right, left + flip, right + flip, far, far + flip)[which]
        at = pl.ds((i % CHUNKS) * step_rows, step_rows)
        ref = whole.at[i // CHUNKS, owner, at]
        remote(ref, ref, send.at[i, which], recv.at[i, which], "tensor", sib).wait_recv()

    def begin(i):
        for which in (1, 2, 0):
            copy(i, which).start()

        @pl.when(i >= live)
        def _():
            at = pl.ds((i % CHUNKS) * step_rows, step_rows)
            ref = whole.at[i // CHUNKS, me, at]
            remote(ref, ref, send.at[i, 5], recv.at[i, 5], "tensor", far).start()

    def relay(i):
        arrived(i, 1)
        arrived(i, 2)
        pl.when(i < live)(lambda: copy(i, 5).start())
        copy(i, 3).start()
        copy(i, 4).start()

    def relay_far(i):
        arrived(i, 5)
        copy(i, 6).start()

    def complete(i):
        for which in (0, 3, 4, 6):
            arrived(i, which)

    coord = [(cx, cz), (cx, cz), (cz, cx), (cz, cx)]
    sign = [1, 3, 1, 3]

    load_emb.wait()
    pl.semaphore_wait(barrier, len(peers))

    @pl.loop(0, CHUNKS)
    def _(i):
        begin(i)

    for h in range(4):
        load_expert(h).start()

    row_id = lax.broadcasted_iota(jnp.int32, mask.shape, 0) % GROUP
    col_id = lax.broadcasted_iota(jnp.int32, mask.shape, 1) % GROUP
    mask[...] = jnp.where(row_id == col_id, 1.0 / math.sqrt(DEMB * NEMB), 0.0)

    load_ids.wait()
    load_gates.wait()
    lane = lax.broadcasted_iota(jnp.int32, (n_dev, rows), 0)
    is_first = (ids[0:1, :] == lane).astype(F32)
    is_second = (ids[1:2, :] == lane).astype(F32)
    member = (is_first + is_second).astype(BF16)
    earlier = (
        lax.broadcasted_iota(jnp.int32, (rows, rows), 0)
        < lax.broadcasted_iota(jnp.int32, (rows, rows), 1)
    ).astype(F32).astype(BF16)
    slot_of = dot(member, earlier) + lane.astype(F32) * cap
    table[...] = jnp.zeros(table.shape, F32)
    table[0:1, :] = jnp.sum(is_first * slot_of, axis=0, keepdims=True)
    table[1:2, :] = jnp.sum(is_second * slot_of, axis=0, keepdims=True)
    for t in range(2):
        table[2 + 2 * t : 4 + 2 * t, :] = gates[t]
    cols[...] = table[...].T

    def gate(at, t, k):
        return cols[at, 2 + 2 * t + k : 3 + 2 * t + k]

    def chosen(expert, k):
        wanted = lax.broadcasted_iota(jnp.int32, (cap, rows), 0) + expert * cap
        return (table[k : k + 1, :].astype(jnp.int32) == wanted).astype(F32).astype(BF16)

    relay(0)
    load_grad.wait()
    every = slice(0, rows)
    for k in range(2):
        cot[k] = (
            gate(every, 0, k) * grad[0].astype(F32) + gate(every, 1, k) * grad[1].astype(F32)
        ).astype(BF16)

    def cotangent(e):
        outg[e] = (dot(chosen(e, 0), cot[0]) + dot(chosen(e, 1), cot[1])).astype(BF16)

    for i in range(1, RELAY):
        relay(i)
    for e in range(4):
        cotangent(e)
    for i in range(FAR):
        relay_far(i)
    load_gains.wait()
    load_weights.wait()

    @pl.loop(0, live)
    def _(i):
        stage, first = i // CHUNKS, (i % CHUNKS) * step_rows
        span = pl.ds(pl.multiple_of(first, step_rows), step_rows)
        complete(i)

        def tile(n):
            return whole[stage, n // 2, span, (n % 2) * DEMB : (n % 2 + 1) * DEMB].astype(F32)

        total = jnp.zeros((step_rows, DEMB), F32)
        for n in range(NEMB):
            x = tile(n)
            total = total + x * x
        mean = jnp.sum(total, axis=1, keepdims=True) / (NEMB * DEMB)
        scale = lax.rsqrt(mean + 1e-05)
        for n in range(NEMB):
            lanes = slice(n * DEMB, (n + 1) * DEMB)
            gain = jnp.where(stage == 0, gains[0:1, lanes], gains[1:2, lanes])
            nrm[n] = (tile(n) * scale * gain).astype(BF16)
        relay(i + RELAY)
        groups = step_rows // GROUP
        for g in range(groups):
            if g == groups // 2:
                relay_far(i + FAR)
            at = slice(g * GROUP, (g + 1) * GROUP)
            stack = nrm[:, at, :].reshape(NEMB * GROUP, DEMB)
            gram = (dot_nt(stack, stack) * mask[...]).astype(BF16)
            mixed = dot(gram, stack).astype(BF16)
            mixed = mixed.reshape(NEMB, GROUP, DEMB)
            for n in range(NEMB):
                inter[at, n * DEMB : (n + 1) * DEMB] = mixed[n]

        pre = dot(inter[...], wheld[stage])
        value = whole[stage, me, span].astype(F32) + pre * jax.nn.sigmoid(pre)
        whole[stage + 1, me, span] = value.astype(BF16)
        begin(i + CHUNKS)

    def to_expert(d):
        to = (me + d) % n_dev
        return remote(outg.at[to], slot_grad.at[me], gsend.at[d], grecv.at[d], "tensor", to)

    for i in range(live, items):
        if i + RELAY < items:
            relay(i + RELAY)
            for e in range(4 + 2 * (i - live), 6 + 2 * (i - live)):
                cotangent(e)
        if i + FAR < items:
            relay_far(i + FAR)

    def send_cotangents():
        @pl.loop(1, n_dev)
        def _(d):
            to_expert(d).start()

    pl.when(core == 0)(send_cotangents)
    for i in range(live, items):
        complete(i)
    slot_grad[me] = outg[me]

    mine = (chosen(me, 0).astype(F32) + chosen(me, 1).astype(F32)).astype(BF16)
    for q in range(n_dev):
        rows_in[:, q * width : (q + 1) * width] = dot(mine, whole[2, q]).astype(BF16)
    eye = (
        lax.broadcasted_iota(jnp.int32, (width, width), 0)
        == lax.broadcasted_iota(jnp.int32, (width, width), 1)
    ).astype(F32).astype(BF16)
    for q in range(n_dev):
        rows_t[q * width : (q + 1) * width, :] = dot_nt(
            eye, rows_in[:, q * width : (q + 1) * width]
        ).astype(BF16)

    def partial(h, t, j):
        u, v = coord[h]
        owner = place(h, (u + (4 - sign[h]) * (1 + t)) % 4, (v + (4 - sign[h]) * (1 + j)) % 4)
        at = pl.ds(pl.multiple_of(owner * piece, piece), piece)
        return dot(rows_t[at, :], pgrad[:, h * part : (h + 1) * part])

    def hop1(h, k, src):
        u, v = coord[h]
        return remote(
            src, ring_buf.at[h, k], send1.at[h, k], recv1.at[h, k],
            "dp", place(h, (u + sign[h]) % 4, v),
        )

    def hop2(h, j):
        u, v = coord[h]
        return remote(
            ring_buf.at[h, 8 + j], last_buf.at[h, j],
            send2.at[h, j], recv2.at[h, j], "dp", place(h, u, (v + sign[h]) % 4),
        )

    def hop0(h, j, sub):
        u, v = coord[h]
        return remote(
            first_buf.at[h, sub, j], ring_buf.at[h, j, :, pl.ds(sub * width, width)],
            send0.at[h, sub, j], recv0.at[h, sub, j], "dp", place(h, (u + sign[h]) % 4, v),
        )

    for sub in range(2):
        for p in range(sub, n_dev, 2):
            if sub == 0:
                load_expert(p // 2).wait()
            pre = dot(rows_in[...], held[:, p * width : (p + 1) * width])
            sigma = jax.nn.sigmoid(pre)
            outs[p] = (pre * sigma).astype(BF16)
            slopes[p] = sigma + pre * sigma * (1.0 - sigma)
        if sub == 0:
            pl.when(core == 1)(send_cotangents)

        @pl.loop(1, n_dev)
        def _(d):
            source = (me + n_dev - d) % n_dev

            @pl.when(source % 2 == sub)
            def _():
                remote(
                    outg.at[me], slot_grad.at[source], gsend.at[d], grecv.at[d], "tensor", source
                ).wait_recv()

        for h in range(4):
            p = 2 * h + sub
            lanes = slice(p * width, (p + 1) * width)
            pgrad[:, lanes] = (slot_grad[p].astype(F32) * slopes[p]).astype(BF16)
            u, v = coord[h]

            @pl.loop(0, 4)
            def _(j):
                owner = place(h, (u + 4 - sign[h]) % 4, (v + (4 - sign[h]) * (1 + j)) % 4)
                at = pl.ds(pl.multiple_of(owner * piece, piece), piece)
                first_buf[h, sub, j] = dot(rows_t[at, :], pgrad[:, lanes]).astype(BF16)
                hop0(h, j, sub).start()

    def out_copy(d):
        to = (me + d) % n_dev
        return remote(outs.at[to], ret.at[me], osend.at[d], orecv.at[d], "tensor", to)

    @pl.loop(1, n_dev)
    def _(d):
        out_copy(d).start()

    ret[me] = outs[me]

    def ring_step(k, arrive):
        t, j = k // 4, k % 4
        own = [partial(h, t, j) for h in range(4)]
        for h in range(4):
            arrive(h, k - 4)
            ring_buf[h, k - 4] = (ring_buf[h, k - 4].astype(F32) + own[h]).astype(BF16)
            hop1(h, k, ring_buf.at[h, k - 4]).start()

    @pl.loop(4, 8)
    def _(k):
        def arrive(h, j):
            for sub in range(2):
                hop0(h, j, sub).wait_recv()

        ring_step(k, arrive)

    @pl.loop(1, n_dev)
    def _(d):
        source = (me + n_dev - d) % n_dev
        remote(
            outs.at[me], ret.at[source], osend.at[d], orecv.at[d], "tensor", source
        ).wait_recv()

    block_rows = 128

    @pl.loop(0, rows // block_rows)
    def _(b):
        at = pl.ds(pl.multiple_of(b * block_rows, block_rows), block_rows)
        seat = lax.broadcasted_iota(jnp.int32, (block_rows, cap), 1)
        picked = []
        for k in range(2):
            slot = cols[at, k : k + 1].astype(jnp.int32)
            total = jnp.zeros((block_rows, width), F32)
            for e in range(n_dev):
                hot = (slot == seat + e * cap).astype(F32).astype(BF16)
                total = total + dot(hot, ret[e])
            picked.append(total)
        for t in range(2):
            both = gate(at, t, 0) * picked[0] + gate(at, t, 1) * picked[1]
            mix[t, at, :] = both.astype(BF16)

    store_mix = pltpu.make_async_copy(mix, mix_out, lsem.at[0])
    store_mix.start()

    def store_wgrad(h):
        span = pl.ds(h * part, part)
        return pltpu.make_async_copy(wgrad.at[:, span], wgrad_out.at[:, span], wsem.at[h])

    @pl.loop(8, 12)
    def _(k):
        ring_step(k, lambda h, j: hop1(h, j, ring_buf.at[h, j]).wait_recv())

    for j in range(4):
        own = [partial(h, 3, j) for h in range(4)]
        for h in range(4):
            hop1(h, 8 + j, ring_buf.at[h, 8 + j]).wait_recv()
            total = ring_buf[h, 8 + j].astype(F32) + own[h]
            if j > 0:
                hop2(h, j - 1).wait_recv()
                total = total + last_buf[h, j - 1].astype(F32)
            if j < 3:
                ring_buf[h, 8 + j] = total.astype(BF16)
                hop2(h, j).start()
            else:
                wgrad[:, h * part : (h + 1) * part] = total
                store_wgrad(h).start()

    store_mix.wait()
    for h in range(4):
        store_wgrad(h).wait()

    @pl.loop(0, items)
    def _(i):
        for which in range(7):
            copy(i, which).wait_send()

    for h in range(4):
        @pl.loop(0, 4)
        def _(j):
            for sub in range(2):
                hop0(h, j, sub).wait_send()

        @pl.loop(4, 12)
        def _(k):
            hop1(h, k, ring_buf.at[h, k - 4]).wait_send()

        for j in range(3):
            hop2(h, j).wait_send()

    @pl.loop(1, n_dev)
    def _(d):
        to_expert(d).wait_send()
        out_copy(d).wait_send()


HBM = pl.BlockSpec(memory_space=pltpu.HBM)
DMA = pltpu.SemaphoreType.DMA


def on_device(
    embeddings, trunk_weights, trunk_gains, expert_weights, route_ids, task_gates, mixture_grad
):
    experts = lax.axis_size("tensor")
    rows, top = route_ids.shape
    cap = 2 * rows * top // experts
    width = embeddings.shape[1]
    full = width * experts
    step_rows = rows // CHUNKS
    piece = full // lax.axis_size("dp")
    by_slot = (experts, cap, width)

    mixture, weight_grad = pl.pallas_call(
        kernel,
        out_shape=(
            jax.ShapeDtypeStruct((2, rows, width), BF16),
            jax.ShapeDtypeStruct((piece, full), F32),
        ),
        in_specs=[HBM] * 7,
        out_specs=(HBM, HBM),
        scratch_shapes=[
            pltpu.VMEM((3, experts, rows, width), BF16),
            pltpu.VMEM((NEMB, step_rows, DEMB), BF16),
            pltpu.VMEM((step_rows, full), BF16),
            pltpu.VMEM((NEMB * GROUP, NEMB * GROUP), F32),
            pltpu.VMEM((2, full, width), BF16),
            pltpu.VMEM((2, rows, width), BF16),
            pltpu.VMEM((2, full), F32),
            pltpu.VMEM((top, rows), jnp.int32),
            pltpu.VMEM((2, top, rows), F32),
            pltpu.VMEM((2, rows, width), BF16),
            pltpu.VMEM(by_slot, BF16),
            pltpu.VMEM(by_slot, BF16),
            pltpu.VMEM((128, rows), F32),
            pltpu.VMEM((rows, 128), F32),
            pltpu.VMEM((full, full), BF16),
            pltpu.VMEM((cap, full), BF16),
            pltpu.VMEM((full, cap), BF16),
            pltpu.VMEM(by_slot, F32),
            pltpu.VMEM((cap, full), BF16),
            pltpu.VMEM(by_slot, BF16),
            pltpu.VMEM(by_slot, BF16),
            pltpu.VMEM((4, 2, 4, piece, width), BF16),
            pltpu.VMEM((4, 12, piece, full // 4), BF16),
            pltpu.VMEM((4, 3, piece, full // 4), BF16),
            pltpu.VMEM((2, rows, width), BF16),
            pltpu.VMEM((piece, full), F32),
            DMA((6,)),
            DMA((4,)),
            DMA((3 * CHUNKS, 7)),
            DMA((3 * CHUNKS, 7)),
            DMA((experts,)),
            DMA((experts,)),
            DMA((4, 12)),
            DMA((4, 12)),
            DMA((4, 3)),
            DMA((4, 3)),
            DMA((experts,)),
            DMA((experts,)),
            DMA((4, 2, 4)),
            DMA((4, 2, 4)),
        ],
        compiler_params=pltpu.CompilerParams(
            collective_id=0, has_side_effects=True, vmem_limit_bytes=56 << 20
        ),
        cost_estimate=pl.CostEstimate(flops=12 << 30, bytes_accessed=16 << 20, transcendentals=0),
        name="trunk_experts",
    )(
        embeddings, trunk_gains, trunk_weights, expert_weights[0], route_ids.T,
        task_gates.transpose(1, 2, 0), mixture_grad,
    )
    return (mixture, weight_grad[None])


def solution(mesh):
    in_specs = (
        P("dp", "tensor"),
        P(None, None, "tensor"),
        P(),
        P("tensor", None, None),
        P("dp", None),
        P("dp", None, None),
        P(None, "dp", "tensor"),
    )
    out_specs = (P(None, "dp", "tensor"), P("tensor", "dp", None))
    return jax.shard_map(
        on_device, mesh=mesh, in_specs=in_specs, out_specs=out_specs, check_vma=False
    )
```
